512 devices in a mesh: pair: 32 (over y, z_hi, core), tm: 16 (over z_lo, x).
Axes of the slice: x: 4, y: 4, z: 16 (z_hi: 4, z_lo: 4; z = z_hi * 4 + z_lo), core: 2. Of those that a mesh axis runs over, the one named last changes fastest.
Arguments:
- samples: float32 [2048, 16384], P('pair', 'tm'), may hold values from -1100 to 1100
- tile_rows: int32 [128], replicated, may hold values from 0 to 63, as said below
- tile_offsets: int32 [128], replicated, may hold values from -31 to 31
- tile_live: int32 [128], replicated, may hold values from 0 to 1, as said below
Outputs:
- correlations: float32 [128, 256, 1024], P('pair', 'tm')
The draws below stay inside these ranges and needn't reach their ends.
Inputs may be any that keep to these rules, and one draw needn't show every extreme that they name: `tile_rows`: blocks a and a + offset of a tile lie in 0 to 63 and fewer than 32 apart. Block q belongs to index q // 2 of pair. The live tiles of one index of pair name different blocks, at most 1 of them held by any one index of pair, and in every draw some index names exactly 1 held by one index. `tile_live`: slots are live from the first slot of an index of pair onward; every index has at least 2 live slots and some index has all 4 live.
All inputs are finite; a program needn't handle non-finite values.
Results may differ from the reference program's by a relative error of at most 0.02.
Values may be sent and summed in bfloat16 or wider, within the bound.
No kernel may reach another device: no remote copies, remote signals or barrier semaphores. Data moves between devices by JAX's collectives and lax.ppermute only.
A program may use at most 64 MiB of HBM per device.

```python
import math
import jax
import jax.numpy as jnp
from jax import lax

C = 2048
CB = 32
BAND = 32
LAG = 128
T_DEV = 1024
TD = 4
S = 16384
NLAG = 256
TILES = 128
N_TM = 16


def tile_plan(key):
    subkeys = jax.random.split(jax.random.fold_in(key, 7), 8)
    pair_count = TILES // TD
    per_owner = C // (CB * pair_count)
    owner_span = BAND // per_owner
    capacity = (2 * TD + owner_span - 1) // owner_span
    first_owner = jax.random.randint(subkeys[0], (pair_count,), 0, pair_count - owner_span + 1)
    owner_order = jax.vmap(lambda k: jax.random.permutation(k, owner_span))(jax.random.split(subkeys[1], pair_count)).astype(jnp.int32)
    copy_order = jax.vmap(lambda k: jax.random.permutation(k, per_owner))(jax.random.split(subkeys[2], pair_count * owner_span)).astype(jnp.int32)
    copy_order = copy_order.reshape(pair_count, owner_span, per_owner)
    top_index = jax.random.randint(subkeys[6], (), 0, pair_count)
    bottom_index = (top_index + 1 + jax.random.randint(subkeys[7], (), 0, pair_count - 1)) % pair_count
    positions = jnp.arange(pair_count, dtype=jnp.int32)
    force_top = positions == top_index
    force_bottom = positions == bottom_index
    forced = force_top | force_bottom
    span_steps = jnp.arange(owner_span, dtype=jnp.int32)
    owner_order = jnp.where(force_top[:, None], (owner_span - 1 + span_steps) % owner_span, jnp.where(force_bottom[:, None], (owner_span - span_steps) % owner_span, owner_order))
    first_owner = jnp.where(force_top, pair_count - owner_span, jnp.where(force_bottom, 0, first_owner))
    copy_steps = jnp.arange(per_owner, dtype=jnp.int32)
    high_copy = (per_owner - 1 + copy_steps) % per_owner
    copy_order = jnp.where(forced[:, None, None] & (owner_order[:, :, None] == owner_span - 1), high_copy[None, None, :], jnp.where(forced[:, None, None], copy_steps[None, None, :], copy_order))
    copy_order = copy_order[:, :, :capacity]
    owners = first_owner[:, None] + owner_order
    blocks_all = owners[:, :, None] * per_owner + copy_order
    blocks_all = jnp.transpose(blocks_all, (0, 2, 1)).reshape(pair_count, capacity * owner_span)
    chosen = blocks_all[:, :2 * TD].reshape(pair_count * TD, 2)
    smaller = jnp.where(jax.random.randint(subkeys[3], (pair_count,), 0, 4) > 0, jax.random.randint(subkeys[4], (pair_count,), TD - 1, TD + 1), 2)
    fullest = jax.random.randint(subkeys[5], (), 0, pair_count)
    live_counts = jnp.where(positions == fullest, TD, smaller)
    alive = (jnp.arange(TD, dtype=jnp.int32)[None, :] < live_counts[:, None]).astype(jnp.int32).reshape(TILES)
    return (chosen[:, 0].astype(jnp.int32), (chosen[:, 1] - chosen[:, 0]).astype(jnp.int32), alive)


def draw_tile_rows(key, part):
    return tile_plan(key)[0]


def draw_tile_offsets(key, part):
    return tile_plan(key)[1]


def draw_tile_live(key, part):
    return tile_plan(key)[2]


def draw_samples(key, part):
    subkeys = jax.random.split(jax.random.fold_in(key, 3), 5)
    fraction = jnp.arange(S, dtype=jnp.float32) / (S - 1)
    ramp = jnp.exp(fraction * math.log(3.0))[None, :]
    rough = jnp.exp(jax.random.uniform(subkeys[1], (1, S), jnp.float32, 0.0, math.log(3.3)))
    offsets = 0.5 * jnp.clip(jax.random.normal(subkeys[4], (C, 1), jnp.float32), -2.0, 2.0)
    gains = jnp.exp(jax.random.uniform(subkeys[0], (C, 1), jnp.float32, 0.0, math.log(10.0)))
    noise = jnp.clip(jax.random.normal(subkeys[2], (C, S), jnp.float32), -6.0, 6.0)
    return (gains * (offsets + ramp * rough * noise)).astype(jnp.float32)


def setup_inputs(seed: int = 0) -> dict:
    splits = jax.random.split(jax.random.key(seed), 5)
    return {
        "samples": draw_samples(jax.random.fold_in(splits[4], 71), 0),
        "tile_rows": draw_tile_rows(jax.random.fold_in(splits[4], 71), 0),
        "tile_offsets": draw_tile_offsets(jax.random.fold_in(splits[4], 71), 0),
        "tile_live": draw_tile_live(jax.random.fold_in(splits[4], 71), 0),
    }


def lag_products(middle, window_rows):
    length = middle.shape[1]
    lag_count = window_rows.shape[1] - length
    middle_wide = middle.astype(jnp.float32)

    def one_block(block_index):

        def one_lag(offset):
            return lax.dynamic_slice_in_dim(window_rows, block_index * 16 + offset, length, 1)
        shifted = jax.vmap(one_lag)(jnp.arange(16, dtype=jnp.int32)).astype(jnp.float32)
        return jnp.einsum('it,ljt->lij', middle_wide, shifted, precision=lax.Precision.HIGHEST)
    blocks_out = lax.map(one_block, jnp.arange(lag_count // 16, dtype=jnp.int32))
    return blocks_out.reshape(lag_count, middle.shape[0] * middle.shape[0])

def reference(samples, tile_rows, tile_offsets, tile_live):
    whole_length = T_DEV * N_TM
    factor = 1.0 / math.sqrt(whole_length)
    average = lax.optimization_barrier(jnp.sum(samples, axis=1)) / whole_length
    power_mean = lax.optimization_barrier(jnp.sum(samples * samples, axis=1)) / whole_length
    scaling = lax.rsqrt(power_mean - average * average + 1e-05)
    whitened = ((samples - average[:, None]) * scaling[:, None]).astype(jnp.bfloat16)
    padded = jnp.pad(whitened, ((0, 0), (LAG, LAG))).reshape(C // CB, CB, whole_length + 2 * LAG)

    def tile_correlation(row_index, offset_value):
        first_block = lax.dynamic_index_in_dim(padded, row_index.astype(jnp.int32), 0, keepdims=False)
        second_block = lax.dynamic_index_in_dim(padded, (row_index + offset_value).astype(jnp.int32), 0, keepdims=False)

        def time_block(accum, block_index):
            start_at = block_index * T_DEV
            middle = lax.dynamic_slice_in_dim(first_block, start_at + LAG, T_DEV, 1)
            window_rows = lax.dynamic_slice_in_dim(second_block, start_at, T_DEV + 2 * LAG, 1)
            term = lag_products(middle, window_rows) * factor
            rounded = lax.optimization_barrier(term.astype(jnp.bfloat16))
            return (accum + rounded.astype(jnp.float32), None)
        initial = jnp.zeros((NLAG, CB * CB), jnp.float32)
        summed, unused = lax.scan(time_block, initial, jnp.arange(N_TM, dtype=jnp.int32))
        return summed

    def one_tile(fields):
        row_index, offset_value, alive = fields
        return lax.cond(alive > 0, lambda: tile_correlation(row_index, offset_value), lambda: jnp.zeros((NLAG, CB * CB), jnp.float32))
    return lax.map(one_tile, (tile_rows, tile_offsets, tile_live))
```

```python
import math

import jax
import jax.numpy as jnp
from jax import lax
from jax.experimental import pallas as pl
from jax.experimental.pallas import tpu as pltpu
from jax.sharding import Mesh
from jax.sharding import PartitionSpec as P

CB = 32
LAG = 128
LANES = 128
Y, ZH, CORE, ZL, X = 4, 4, 2, 4, 4
AXES = ("y", "zh", "core", "zl", "x")
PAIRS = Y * ZH * CORE
TMS = ZL * X
EIGHTHS = Y * CORE
CHUNKS = X * EIGHTHS
FINE = 8
MEDIUM = LANES // FINE
MIB = 1 << 20

VMEM = pl.BlockSpec(memory_space=pltpu.VMEM)
SMEM = pl.BlockSpec(memory_space=pltpu.SMEM)


def whiten_kernel(count, x_ref, sums_ref, out_ref):
    rows = x_ref.shape[0]
    total = jnp.sum(sums_ref[...], axis=0, keepdims=True) / count
    square = pltpu.roll(jnp.broadcast_to(total, (8, LANES)), rows, axis=1)
    first = jnp.broadcast_to(total, (8, LANES))
    scaling = lax.rsqrt(square - first * first + 1e-05)
    row = lax.broadcasted_iota(jnp.int32, (8, LANES), 0)
    both = jnp.where(row == 0, first, scaling)
    turned = jnp.transpose(jnp.concatenate([both] * (LANES // 8), axis=0))
    average = turned[:rows, 0:1]
    scale = turned[:rows, 1:2]
    for part in range(EIGHTHS):
        piece = x_ref[:, part * LANES : (part + 1) * LANES]
        white = ((piece - average) * scale).astype(jnp.bfloat16)
        for zh in range(ZH):
            out_ref[part // CORE, zh, part % CORE] = white


def select_kernel(rows_ref, offsets_ref, table_ref, out_ref):
    zh = lax.axis_index("zh")
    blocks = table_ref.shape[0]

    def one(index, carry):
        place = index // X
        slot = index % X
        pair = (place // CORE * ZH + zh) * CORE + place % CORE
        tile = pair * X + slot
        first = rows_ref[tile]
        second = first + offsets_ref[tile]
        out_ref[2 * index] = table_ref[jnp.clip(first, 0, blocks - 1)]
        out_ref[2 * index + 1] = table_ref[jnp.clip(second, 0, blocks - 1)]
        return carry

    lax.fori_loop(0, EIGHTHS * X, one, 0)


def chunk_place(chunk):
    return chunk % EIGHTHS * X + chunk // EIGHTHS


def lag_kernel(factor, live_ref, data_ref, before_ref, after_ref, out_ref, wide_a, wide_b):
    pair = (lax.axis_index("y") * ZH + lax.axis_index("zh")) * CORE + lax.axis_index("core")
    alive = live_ref[pair * X + lax.axis_index("x")]
    width = (CHUNKS + 1) * LANES

    @pl.when(alive <= 0)
    def _():
        out_ref[...] = jnp.zeros_like(out_ref)

    @pl.when(alive > 0)
    def _():
        lane = lax.broadcasted_iota(jnp.int32, (CB, LANES), 1)
        zero = jnp.zeros((CB, LANES), jnp.float32)

        def first_chunk(chunk):
            return data_ref[chunk_place(chunk), :CB].astype(jnp.float32)

        def second_chunk(chunk):
            if chunk < 0:
                return before_ref[...].astype(jnp.float32)
            if chunk >= CHUNKS:
                return after_ref[...].astype(jnp.float32)
            return data_ref[chunk_place(chunk), CB:].astype(jnp.float32)

        for chunk in range(CHUNKS + 1):
            here = first_chunk(chunk) if chunk < CHUNKS else zero
            past = first_chunk(chunk - 1) if chunk > 0 else zero
            for step in range(MEDIUM):
                shift = step * FINE
                mixed = jnp.where(lane < LANES - shift, here, past)
                turned = pltpu.roll(mixed, shift, axis=1) if shift else here
                wide_a[step * CB : (step + 1) * CB, chunk * LANES : (chunk + 1) * LANES] = (
                    turned.astype(jnp.bfloat16)
                )
        for chunk in range(-1, CHUNKS + 1):
            here = second_chunk(chunk)
            later = second_chunk(chunk + 1) if chunk < CHUNKS else zero
            for step in range(FINE):
                mixed = jnp.where(lane >= step, here, later)
                turned = pltpu.roll(mixed, LANES - step, axis=1) if step else here
                wide_b[
                    step * CB : (step + 1) * CB, (chunk + 1) * LANES : (chunk + 2) * LANES
                ] = turned.astype(jnp.bfloat16)
        for half in range(2):
            result = lax.dot_general(
                wide_a[...],
                wide_b[:, half * LANES : half * LANES + width],
                (((1,), (1,)), ((), ())),
                preferred_element_type=jnp.float32,
            )
            rounded = (result * factor).astype(jnp.bfloat16)
            for part in range(TMS // 2):
                out_ref[half * (TMS // 2) + part] = rounded[part * 2 * CB : (part + 1) * 2 * CB]


def finish_kernel(got_ref, out_ref, grid_ref, turn_ref):
    lane = lax.broadcasted_iota(jnp.int32, (8, LANES), 1)
    for slot in range(X):
        total = got_ref[slot].astype(jnp.float32)
        for zl in range(1, ZL):
            total = total + got_ref[zl * X + slot].astype(jnp.float32)
        for g in range(2):
            grid_ref[g * 2 * CB : (g + 1) * 2 * CB] = total[:, g * LANES : (g + 1) * LANES]
        for half in range(2):
            parts = [
                [
                    grid_ref[pl.ds((2 * g + half) * CB + r, 8, stride=4), :]
                    for g in range(2)
                ]
                for r in range(4)
            ]
            for q in range(FINE):
                line = None
                for r in range(4):
                    piece = parts[r][q // 4]
                    shift = (CB * (r - q % 4)) % LANES
                    piece = pltpu.roll(piece, shift, axis=1) if shift else piece
                    line = piece if line is None else jnp.where(lane >= r * CB, piece, line)
                turn_ref[q * 8 : (q + 1) * 8, :] = line
            for k in range(8):
                out_ref[slot, half * 8 : half * 8 + 8, k * LANES : (k + 1) * LANES] = turn_ref[
                    pl.ds(k, 8, stride=8), :
                ]


def body(samples, tile_rows, tile_offsets, tile_live):
    local_rows, length = samples.shape
    whole_length = length * TMS
    bf16 = jnp.bfloat16
    sums = jnp.concatenate([jnp.sum(samples, axis=1), jnp.sum(samples * samples, axis=1)])
    with jax.named_scope("moments"):
        sums = lax.all_to_all(
            jnp.broadcast_to(sums[None], (TMS, 2 * local_rows)), ("zl", "x"), 0, 0, tiled=True
        )
    white = pl.pallas_call(
        lambda *refs: whiten_kernel(float(whole_length), *refs),
        out_shape=jax.ShapeDtypeStruct((Y, ZH, CORE, local_rows, LANES), bf16),
        in_specs=[VMEM, VMEM],
        out_specs=VMEM,
        name="whiten",
    )(samples, sums)
    with jax.named_scope("spread"):
        table = lax.all_to_all(
            white.reshape(PAIRS, local_rows, LANES), ("y", "zh", "core"), 0, 0, tiled=True
        )
    chosen = pl.pallas_call(
        select_kernel,
        out_shape=jax.ShapeDtypeStruct((CHUNKS * 2, CB, LANES), bf16),
        in_specs=[SMEM, SMEM, VMEM],
        out_specs=VMEM,
        name="select",
    )(tile_rows, tile_offsets, table.reshape(PAIRS * local_rows // CB, CB, LANES))
    with jax.named_scope("collect"):
        data = lax.all_to_all(
            chosen.reshape(CHUNKS, 2 * CB, LANES), ("y", "core", "x"), 0, 0, tiled=True
        )
    with jax.named_scope("halo"):
        before = lax.ppermute(
            data[chunk_place(CHUNKS - 1), CB:], "zl", [(i, i + 1) for i in range(ZL - 1)]
        )
        after = lax.ppermute(data[chunk_place(0), CB:], "zl", [(i + 1, i) for i in range(ZL - 1)])
    partial = pl.pallas_call(
        lambda *refs: lag_kernel(1.0 / math.sqrt(whole_length), *refs),
        out_shape=jax.ShapeDtypeStruct((TMS, 2 * CB, FINE * CB), bf16),
        in_specs=[SMEM, VMEM, VMEM, VMEM],
        out_specs=VMEM,
        scratch_shapes=[
            pltpu.VMEM((MEDIUM * CB, (CHUNKS + 1) * LANES), bf16),
            pltpu.VMEM((FINE * CB, (CHUNKS + 2) * LANES), bf16),
        ],
        compiler_params=pltpu.CompilerParams(vmem_limit_bytes=40 * MIB),
        name="lags",
    )(tile_live, data, before, after)
    with jax.named_scope("reduce"):
        got = lax.all_to_all(partial, ("zl", "x"), 0, 0, tiled=True)
    return pl.pallas_call(
        finish_kernel,
        out_shape=jax.ShapeDtypeStruct((X, 2 * FINE, CB * CB), jnp.float32),
        in_specs=[VMEM],
        out_specs=VMEM,
        scratch_shapes=[
            pltpu.VMEM((4 * CB, LANES), jnp.float32),
            pltpu.VMEM((FINE * 8, LANES), jnp.float32),
        ],
        name="finish",
    )(got)


def solution(mesh):
    devices = mesh.devices.reshape(Y, ZH, CORE, ZL, X)
    spread = Mesh(devices, AXES)
    pair, tm = ("y", "zh", "core"), ("zl", "x")
    return jax.shard_map(
        body,
        mesh=spread,
        in_specs=(P(pair, tm), P(), P(), P()),
        out_specs=P(pair, tm, None),
        check_vma=False,
    )
```

```python
import math

import jax
import jax.numpy as jnp
from jax import lax
from jax.experimental import pallas as pl
from jax.experimental.pallas import tpu as pltpu
from jax.sharding import Mesh
from jax.sharding import PartitionSpec as P

CB = 32
LAG = 128
LANES = 128
Y, ZH, CORE, ZL, X = 4, 4, 2, 4, 4
AXES = ("y", "zh", "core", "zl", "x")
PAIRS = Y * ZH * CORE
TMS = ZL * X
EIGHTHS = Y * CORE
CHUNKS = X * EIGHTHS
FINE = 8
MEDIUM = LANES // FINE
EXTRA = 8
ROWS = 2 * CB + EXTRA
MIB = 1 << 20

VMEM = pl.BlockSpec(memory_space=pltpu.VMEM)
SMEM = pl.BlockSpec(memory_space=pltpu.SMEM)


def split_kernel(x_ref, out_ref, extra_ref):
    rows, length = x_ref.shape
    mean = jnp.sum(x_ref[...], axis=1, keepdims=True) / length
    spread = jnp.zeros((rows, 1), jnp.float32)
    for part in range(EIGHTHS):
        piece = x_ref[:, part * LANES : (part + 1) * LANES] - mean
        spread = spread + jnp.sum(piece * piece, axis=1, keepdims=True)
        out_ref[part] = piece.astype(jnp.bfloat16)
    lane = lax.broadcasted_iota(jnp.int32, (rows, LANES), 1)
    columns = jnp.where(lane == 0, mean, jnp.where(lane == 1, spread, 0.0))
    turned = jnp.transpose(jnp.concatenate([columns] * (LANES // rows), axis=0))
    wide = lax.broadcasted_iota(jnp.int32, (1, LANES), 1)
    line = jnp.where(wide < rows, turned[0:1], turned[1:2])
    high = line.astype(jnp.bfloat16).astype(jnp.float32)
    middle = (line - high).astype(jnp.bfloat16).astype(jnp.float32)
    low = line - high - middle
    row = lax.broadcasted_iota(jnp.int32, (EXTRA, LANES), 0) % (EXTRA // 2)
    lines = jnp.where(row == 0, high, jnp.where(row == 1, middle, jnp.where(row == 2, low, 0.0)))
    extra_ref[...] = lines.astype(jnp.bfloat16)


def select_kernel(rows_ref, offsets_ref, table_ref, out_ref):
    zh = lax.axis_index("zh")
    here = lax.axis_index("y") * CORE + lax.axis_index("core")
    bulk = EIGHTHS * 2 * CB
    row = lax.broadcasted_iota(jnp.int32, (EXTRA, LANES), 0)

    def fetch(block):
        block = jnp.clip(block, 0, 2 * PAIRS - 1)
        place = ((block >> 4) << 1) | ((block >> 1) & 1)
        column = (block >> 2) & (ZH - 1)
        start = pl.multiple_of(((place << 1) | (block & 1)) * CB, CB)
        data = table_ref[column, pl.ds(start, CB)]
        lines = table_ref[column, bulk:]
        lines = jnp.where(place == here, lines, jnp.zeros_like(lines))
        return data, lines

    def one(index, carry):
        place = index >> 2
        pair = (((place >> 1) * ZH + zh) << 1) | (place & 1)
        tile = pair * X + (index & (X - 1))
        first = rows_ref[tile]
        data, lines = fetch(first)
        data_second, lines_second = fetch(first + offsets_ref[tile])
        out_ref[index, :CB] = data
        out_ref[index, CB : 2 * CB] = data_second
        out_ref[index, 2 * CB :] = jnp.where(row < EXTRA // 2, lines, lines_second)
        return carry

    lax.fori_loop(0, EIGHTHS * X, one, 0, unroll=4)


def chunk_place(chunk):
    return chunk % EIGHTHS * X + chunk // EIGHTHS


def scales(edge_ref, side, half, zl, length):
    lines = []
    for part in range(TMS):
        start = 2 * CB + part % X * EXTRA
        lines.append(edge_ref[part // X, start : start + EXTRA].astype(jnp.float32))
    base = side * (EXTRA // 2)
    sums = [line[base : base + 1] + (line[base + 1 : base + 2] + line[base + 2 : base + 3]) for line in lines]
    sums = jnp.concatenate(sums, axis=0)
    sums = jnp.where(half > 0, pltpu.roll(sums, LANES - CB, axis=1), sums)
    squares = jnp.sum(pltpu.roll(sums, LANES // 2, axis=1), axis=0, keepdims=True)
    apart = sums - jnp.sum(sums, axis=0, keepdims=True) / TMS
    power = (squares / length + jnp.sum(apart * apart, axis=0, keepdims=True)) / TMS
    scaling = lax.rsqrt(power + 1e-05)
    place = lax.broadcasted_iota(jnp.int32, (TMS, LANES), 0)
    row = lax.broadcasted_iota(jnp.int32, (8, LANES), 0)
    packed = jnp.broadcast_to(scaling, (8, LANES))
    for column in range(X + 2):
        wanted = zl * X + column - 1
        one = jnp.sum(jnp.where(place == wanted, apart, 0.0), axis=0, keepdims=True)
        packed = jnp.where(row == column + 1, one, packed)
    lane = lax.broadcasted_iota(jnp.int32, (8, LANES), 1)
    packed = jnp.where(lane < CB, packed, 0.0)
    return jnp.transpose(jnp.concatenate([packed] * (LANES // 8), axis=0))[:CB, :8]


def lag_kernel(length, rows_ref, offsets_ref, live_ref, data_ref, edge_ref, out_ref, wide_a, wide_b):
    zl = lax.axis_index("zl")
    pair = (lax.axis_index("y") * ZH + lax.axis_index("zh")) * CORE + lax.axis_index("core")
    tile = pair * X + lax.axis_index("x")
    alive = live_ref[tile]
    first_half = lax.rem(rows_ref[tile], 2)
    second_half = lax.rem(rows_ref[tile] + offsets_ref[tile] + PAIRS * 2, 2)
    width = (CHUNKS + 1) * LANES
    factor = 1.0 / math.sqrt(length * TMS)

    @pl.when(alive <= 0)
    def _():
        out_ref[...] = jnp.zeros_like(out_ref)

    @pl.when(alive > 0)
    def _():
        lane = lax.broadcasted_iota(jnp.int32, (CB, LANES), 1)
        zero = jnp.zeros((CB, LANES), jnp.float32)
        first_scale = scales(edge_ref, 0, first_half, zl, length)
        second_scale = scales(edge_ref, 1, second_half, zl, length)

        def white(piece, scale, column):
            shifted = piece.astype(jnp.float32) + scale[:, column + 2 : column + 3]
            return shifted * scale[:, 0:1]

        def first_chunk(chunk):
            return white(data_ref[chunk_place(chunk), :CB], first_scale, chunk // EIGHTHS)

        def second_chunk(chunk):
            if chunk < 0:
                piece = white(edge_ref[jnp.maximum(zl - 1, 0), CB : 2 * CB], second_scale, -1)
                return jnp.where(zl > 0, piece, 0.0)
            if chunk >= CHUNKS:
                piece = white(edge_ref[jnp.minimum(zl + 1, ZL - 1), :CB], second_scale, X)
                return jnp.where(zl < ZL - 1, piece, 0.0)
            return white(data_ref[chunk_place(chunk), CB : 2 * CB], second_scale, chunk // EIGHTHS)

        here = zero
        for chunk in range(CHUNKS + 1):
            past = here
            here = first_chunk(chunk) if chunk < CHUNKS else zero
            for step in range(MEDIUM):
                shift = step * FINE
                mixed = jnp.where(lane < LANES - shift, here, past)
                turned = pltpu.roll(mixed, shift, axis=1) if shift else here
                wide_a[step * CB : (step + 1) * CB, chunk * LANES : (chunk + 1) * LANES] = (
                    turned.astype(jnp.bfloat16)
                )
        later = second_chunk(-1)
        for chunk in range(-1, CHUNKS + 1):
            here = later
            later = second_chunk(chunk + 1) if chunk < CHUNKS else zero
            for step in range(FINE):
                mixed = jnp.where(lane >= step, here, later)
                turned = pltpu.roll(mixed, LANES - step, axis=1) if step else here
                wide_b[
                    step * CB : (step + 1) * CB, (chunk + 1) * LANES : (chunk + 2) * LANES
                ] = turned.astype(jnp.bfloat16)
        for half in range(2):
            result = lax.dot_general(
                wide_a[...],
                wide_b[:, half * LANES : half * LANES + width],
                (((1,), (1,)), ((), ())),
                preferred_element_type=jnp.float32,
            )
            rounded = (result * factor).astype(jnp.bfloat16)
            for part in range(TMS // 2):
                out_ref[half * (TMS // 2) + part] = rounded[part * 2 * CB : (part + 1) * 2 * CB]


def finish_kernel(got_ref, out_ref, grid_ref, turn_ref):
    lane = lax.broadcasted_iota(jnp.int32, (8, LANES), 1)
    for slot in range(X):
        total = got_ref[slot].astype(jnp.float32)
        for zl in range(1, ZL):
            total = total + got_ref[zl * X + slot].astype(jnp.float32)
        for g in range(2):
            grid_ref[g * 2 * CB : (g + 1) * 2 * CB] = total[:, g * LANES : (g + 1) * LANES]
        for half in range(2):
            parts = [
                [
                    grid_ref[pl.ds((2 * g + half) * CB + r, 8, stride=4), :]
                    for g in range(2)
                ]
                for r in range(4)
            ]
            for q in range(FINE):
                line = None
                for r in range(4):
                    piece = parts[r][q // 4]
                    shift = (CB * (r - q % 4)) % LANES
                    piece = pltpu.roll(piece, shift, axis=1) if shift else piece
                    line = piece if line is None else jnp.where(lane >= r * CB, piece, line)
                turn_ref[q * 8 : (q + 1) * 8, :] = line
            for k in range(8):
                out_ref[slot, half * 8 : half * 8 + 8, k * LANES : (k + 1) * LANES] = turn_ref[
                    pl.ds(k, 8, stride=8), :
                ]


def body(samples, tile_rows, tile_offsets, tile_live):
    length = samples.shape[1]
    bf16 = jnp.bfloat16
    parts, lines = pl.pallas_call(
        split_kernel,
        out_shape=(
            jax.ShapeDtypeStruct((EIGHTHS, 2 * CB, LANES), bf16),
            jax.ShapeDtypeStruct((EXTRA, LANES), bf16),
        ),
        in_specs=[VMEM],
        out_specs=(VMEM, VMEM),
        name="split",
    )(samples)
    with jax.named_scope("spread_y"):
        table = lax.all_to_all(parts, ("y", "core"), 0, 0, tiled=True)
    with jax.named_scope("spread_z"):
        table = jnp.concatenate([table.reshape(EIGHTHS * 2 * CB, LANES), lines])
        table = lax.all_gather(table, "zh")
    chosen = pl.pallas_call(
        select_kernel,
        out_shape=jax.ShapeDtypeStruct((CHUNKS, ROWS, LANES), bf16),
        in_specs=[SMEM, SMEM, VMEM],
        out_specs=VMEM,
        name="select",
    )(tile_rows, tile_offsets, table)
    with jax.named_scope("collect"):
        data = lax.all_to_all(chosen, ("y", "core", "x"), 0, 0, tiled=True)
    with jax.named_scope("edges"):
        sums = jnp.sum(data[:, 2 * CB :].reshape(EIGHTHS, X * EXTRA, LANES), axis=0)
        edges = jnp.concatenate(
            [data[chunk_place(0), CB : 2 * CB], data[chunk_place(CHUNKS - 1), CB : 2 * CB], sums]
        )
        edges = lax.all_to_all(
            jnp.broadcast_to(edges[None], (ZL,) + edges.shape), "zl", 0, 0, tiled=True
        )
    partial = pl.pallas_call(
        lambda *refs: lag_kernel(length, *refs),
        out_shape=jax.ShapeDtypeStruct((TMS, 2 * CB, FINE * CB), bf16),
        in_specs=[SMEM, SMEM, SMEM, VMEM, VMEM],
        out_specs=VMEM,
        scratch_shapes=[
            pltpu.VMEM((MEDIUM * CB, (CHUNKS + 1) * LANES), bf16),
            pltpu.VMEM((FINE * CB, (CHUNKS + 2) * LANES), bf16),
        ],
        compiler_params=pltpu.CompilerParams(vmem_limit_bytes=40 * MIB),
        name="lags",
    )(tile_rows, tile_offsets, tile_live, data, edges)
    with jax.named_scope("reduce"):
        got = lax.all_to_all(partial, ("zl", "x"), 0, 0, tiled=True)
    return pl.pallas_call(
        finish_kernel,
        out_shape=jax.ShapeDtypeStruct((X, 2 * FINE, CB * CB), jnp.float32),
        in_specs=[VMEM],
        out_specs=VMEM,
        scratch_shapes=[
            pltpu.VMEM((4 * CB, LANES), jnp.float32),
            pltpu.VMEM((FINE * 8, LANES), jnp.float32),
        ],
        name="finish",
    )(got)


def solution(mesh):
    devices = mesh.devices.reshape(Y, ZH, CORE, ZL, X)
    spread = Mesh(devices, AXES)
    pair, tm = ("y", "zh", "core"), ("zl", "x")
    return jax.shard_map(
        body,
        mesh=spread,
        in_specs=(P(pair, tm), P(), P(), P()),
        out_specs=P(pair, tm, None),
        check_vma=False,
    )
```

```python
import math

import jax
import jax.numpy as jnp
from jax import lax
from jax.experimental import pallas as pl
from jax.experimental.pallas import tpu as pltpu
from jax.sharding import Mesh
from jax.sharding import PartitionSpec as P

CB = 32
LAG = 128
LANES = 128
Y, ZH, CORE, ZL, X = 4, 4, 2, 4, 4
AXES = ("y", "zh", "core", "zl", "x")
PAIRS = Y * ZH * CORE
TMS = ZL * X
EIGHTHS = Y * CORE
CHUNKS = X * EIGHTHS
FINE = 8
MEDIUM = LANES // FINE
EXTRA = 8
ROWS = 2 * CB + EXTRA
MIB = 1 << 20

VMEM = pl.BlockSpec(memory_space=pltpu.VMEM)
SMEM = pl.BlockSpec(memory_space=pltpu.SMEM)


def split_kernel(x_ref, out_ref, extra_ref):
    rows, length = x_ref.shape
    mean = jnp.sum(x_ref[...], axis=1, keepdims=True) / length
    spread = jnp.zeros((rows, 1), jnp.float32)
    for part in range(EIGHTHS):
        piece = x_ref[:, part * LANES : (part + 1) * LANES] - mean
        spread = spread + jnp.sum(piece * piece, axis=1, keepdims=True)
        out_ref[part] = piece.astype(jnp.bfloat16)
    lane = lax.broadcasted_iota(jnp.int32, (rows, LANES), 1)
    columns = jnp.where(lane == 0, mean, jnp.where(lane == 1, spread, 0.0))
    turned = jnp.transpose(jnp.concatenate([columns] * (LANES // rows), axis=0))
    wide = lax.broadcasted_iota(jnp.int32, (1, LANES), 1)
    line = jnp.where(wide < rows, turned[0:1], turned[1:2])
    high = line.astype(jnp.bfloat16).astype(jnp.float32)
    middle = (line - high).astype(jnp.bfloat16).astype(jnp.float32)
    low = line - high - middle
    row = lax.broadcasted_iota(jnp.int32, (EXTRA, LANES), 0) % (EXTRA // 2)
    lines = jnp.where(row == 0, high, jnp.where(row == 1, middle, jnp.where(row == 2, low, 0.0)))
    extra_ref[...] = lines.astype(jnp.bfloat16)


def select_kernel(rows_ref, offsets_ref, table_ref, out_ref):
    zh = lax.axis_index("zh")
    here = lax.axis_index("y") * CORE + lax.axis_index("core")
    bulk = EIGHTHS * 2 * CB
    row = lax.broadcasted_iota(jnp.int32, (EXTRA, LANES), 0)

    def fetch(block):
        block = jnp.clip(block, 0, 2 * PAIRS - 1)
        place = ((block >> 4) << 1) | ((block >> 1) & 1)
        column = (block >> 2) & (ZH - 1)
        start = pl.multiple_of(((place << 1) | (block & 1)) * CB, CB)
        data = table_ref[column, pl.ds(start, CB)]
        lines = table_ref[column, bulk:]
        lines = jnp.where(place == here, lines, jnp.zeros_like(lines))
        return data, lines

    def one(index, carry):
        place = index >> 2
        pair = (((place >> 1) * ZH + zh) << 1) | (place & 1)
        tile = pair * X + (index & (X - 1))
        first = rows_ref[tile]
        data, lines = fetch(first)
        data_second, lines_second = fetch(first + offsets_ref[tile])
        out_ref[index, :CB] = data
        out_ref[index, CB : 2 * CB] = data_second
        out_ref[index, 2 * CB :] = jnp.where(row < EXTRA // 2, lines, lines_second)
        return carry

    lax.fori_loop(0, EIGHTHS * X, one, 0, unroll=4)


def chunk_place(chunk):
    return chunk % EIGHTHS * X + chunk // EIGHTHS


def scales(edge_ref, side, half, zl, length):
    lines = []
    for part in range(TMS):
        start = 2 * CB + part % X * EXTRA
        lines.append(edge_ref[part // X, start : start + EXTRA].astype(jnp.float32))
    base = side * (EXTRA // 2)
    sums = [line[base : base + 1] + (line[base + 1 : base + 2] + line[base + 2 : base + 3]) for line in lines]
    sums = jnp.concatenate(sums, axis=0)
    sums = jnp.where(half > 0, pltpu.roll(sums, LANES - CB, axis=1), sums)
    squares = jnp.sum(pltpu.roll(sums, LANES // 2, axis=1), axis=0, keepdims=True)
    apart = sums - jnp.sum(sums, axis=0, keepdims=True) / TMS
    power = (squares / length + jnp.sum(apart * apart, axis=0, keepdims=True)) / TMS
    scaling = lax.rsqrt(power + 1e-05)
    place = lax.broadcasted_iota(jnp.int32, (TMS, LANES), 0)
    row = lax.broadcasted_iota(jnp.int32, (8, LANES), 0)
    packed = jnp.broadcast_to(scaling, (8, LANES))
    for column in range(X + 2):
        wanted = zl * X + column - 1
        one = jnp.sum(jnp.where(place == wanted, apart, 0.0), axis=0, keepdims=True)
        packed = jnp.where(row == column + 1, one, packed)
    lane = lax.broadcasted_iota(jnp.int32, (8, LANES), 1)
    packed = jnp.where(lane < CB, packed, 0.0)
    return jnp.transpose(jnp.concatenate([packed] * (LANES // 8), axis=0))[:CB, :8]


def lag_kernel(length, rows_ref, offsets_ref, live_ref, data_ref, edge_ref, out_ref, wide_a, wide_b):
    zl = lax.axis_index("zl")
    pair = (lax.axis_index("y") * ZH + lax.axis_index("zh")) * CORE + lax.axis_index("core")
    tile = pair * X + lax.axis_index("x")
    alive = live_ref[tile]
    first_half = lax.rem(rows_ref[tile], 2)
    second_half = lax.rem(rows_ref[tile] + offsets_ref[tile] + PAIRS * 2, 2)
    width = (CHUNKS + 1) * LANES
    factor = 1.0 / math.sqrt(length * TMS)

    @pl.when(alive <= 0)
    def _():
        out_ref[...] = jnp.zeros_like(out_ref)

    @pl.when(alive > 0)
    def _():
        lane = lax.broadcasted_iota(jnp.int32, (CB, LANES), 1)
        zero = jnp.zeros((CB, LANES), jnp.bfloat16)
        first_scale = scales(edge_ref, 0, first_half, zl, length)
        second_scale = scales(edge_ref, 1, second_half, zl, length)

        def white(piece, scale, column):
            shifted = piece.astype(jnp.float32) + scale[:, column + 2 : column + 3]
            return (shifted * scale[:, 0:1]).astype(jnp.bfloat16)

        def first_chunk(chunk):
            return white(data_ref[chunk_place(chunk), :CB], first_scale, chunk // EIGHTHS)

        def second_chunk(chunk):
            if chunk < 0:
                piece = white(edge_ref[jnp.maximum(zl - 1, 0), CB : 2 * CB], second_scale, -1)
                return jnp.where(zl > 0, piece, zero)
            if chunk >= CHUNKS:
                piece = white(edge_ref[jnp.minimum(zl + 1, ZL - 1), :CB], second_scale, X)
                return jnp.where(zl < ZL - 1, piece, zero)
            return white(data_ref[chunk_place(chunk), CB : 2 * CB], second_scale, chunk // EIGHTHS)

        here = zero
        for chunk in range(CHUNKS + 1):
            past = here
            here = first_chunk(chunk) if chunk < CHUNKS else zero
            for step in range(MEDIUM):
                shift = step * FINE
                mixed = jnp.where(lane < LANES - shift, here, past)
                turned = pltpu.roll(mixed, shift, axis=1) if shift else here
                wide_a[step * CB : (step + 1) * CB, chunk * LANES : (chunk + 1) * LANES] = turned
        later = second_chunk(-1)
        for chunk in range(-1, CHUNKS + 1):
            here = later
            later = second_chunk(chunk + 1) if chunk < CHUNKS else zero
            for step in range(FINE):
                mixed = jnp.where(lane >= step, here, later)
                turned = pltpu.roll(mixed, LANES - step, axis=1) if step else here
                wide_b[
                    step * CB : (step + 1) * CB, (chunk + 1) * LANES : (chunk + 2) * LANES
                ] = turned
        for half in range(2):
            result = lax.dot_general(
                wide_a[...],
                wide_b[:, half * LANES : half * LANES + width],
                (((1,), (1,)), ((), ())),
                preferred_element_type=jnp.float32,
            )
            rounded = (result * factor).astype(jnp.bfloat16)
            for part in range(TMS // 2):
                out_ref[half * (TMS // 2) + part] = rounded[part * 2 * CB : (part + 1) * 2 * CB]


def finish_kernel(got_ref, out_ref, grid_ref, turn_ref):
    lane = lax.broadcasted_iota(jnp.int32, (8, LANES), 1)
    for slot in range(X):
        total = got_ref[slot].astype(jnp.float32)
        for zl in range(1, ZL):
            total = total + got_ref[zl * X + slot].astype(jnp.float32)
        for g in range(2):
            grid_ref[g * 2 * CB : (g + 1) * 2 * CB] = total[:, g * LANES : (g + 1) * LANES]
        for half in range(2):
            parts = [
                [
                    grid_ref[pl.ds((2 * g + half) * CB + r, 8, stride=4), :]
                    for g in range(2)
                ]
                for r in range(4)
            ]
            for q in range(FINE):
                line = None
                for r in range(4):
                    piece = parts[r][q // 4]
                    shift = (CB * (r - q % 4)) % LANES
                    piece = pltpu.roll(piece, shift, axis=1) if shift else piece
                    line = piece if line is None else jnp.where(lane >= r * CB, piece, line)
                turn_ref[q * 8 : (q + 1) * 8, :] = line
            for k in range(8):
                out_ref[slot, half * 8 : half * 8 + 8, k * LANES : (k + 1) * LANES] = turn_ref[
                    pl.ds(k, 8, stride=8), :
                ]


def body(samples, tile_rows, tile_offsets, tile_live):
    length = samples.shape[1]
    bf16 = jnp.bfloat16
    parts, lines = pl.pallas_call(
        split_kernel,
        out_shape=(
            jax.ShapeDtypeStruct((EIGHTHS, 2 * CB, LANES), bf16),
            jax.ShapeDtypeStruct((EXTRA, LANES), bf16),
        ),
        in_specs=[VMEM],
        out_specs=(VMEM, VMEM),
        compiler_params=pltpu.CompilerParams(vmem_limit_bytes=3 * MIB),
        name="split",
    )(samples)
    with jax.named_scope("spread_y"):
        table = lax.all_to_all(parts, ("y", "core"), 0, 0, tiled=True)
    with jax.named_scope("spread_z"):
        table = jnp.concatenate([table.reshape(EIGHTHS * 2 * CB, LANES), lines])
        table = lax.all_gather(table, "zh")
    chosen = pl.pallas_call(
        select_kernel,
        out_shape=jax.ShapeDtypeStruct((CHUNKS, ROWS, LANES), bf16),
        in_specs=[SMEM, SMEM, VMEM],
        out_specs=VMEM,
        compiler_params=pltpu.CompilerParams(vmem_limit_bytes=6 * MIB),
        name="select",
    )(tile_rows, tile_offsets, table)
    with jax.named_scope("collect"):
        data = lax.all_to_all(chosen, ("y", "core", "x"), 0, 0, tiled=True)
    with jax.named_scope("edges"):
        sums = jnp.sum(data[:, 2 * CB :].reshape(EIGHTHS, X * EXTRA, LANES), axis=0)
        edges = jnp.concatenate(
            [data[chunk_place(0), CB : 2 * CB], data[chunk_place(CHUNKS - 1), CB : 2 * CB], sums]
        )
        edges = lax.all_to_all(
            jnp.broadcast_to(edges[None], (ZL,) + edges.shape), "zl", 0, 0, tiled=True
        )
    partial = pl.pallas_call(
        lambda *refs: lag_kernel(length, *refs),
        out_shape=jax.ShapeDtypeStruct((TMS, 2 * CB, FINE * CB), bf16),
        in_specs=[SMEM, SMEM, SMEM, VMEM, VMEM],
        out_specs=VMEM,
        scratch_shapes=[
            pltpu.VMEM((MEDIUM * CB, (CHUNKS + 1) * LANES), bf16),
            pltpu.VMEM((FINE * CB, (CHUNKS + 2) * LANES), bf16),
        ],
        compiler_params=pltpu.CompilerParams(vmem_limit_bytes=16 * MIB),
        name="lags",
    )(tile_rows, tile_offsets, tile_live, data, edges)
    with jax.named_scope("reduce"):
        got = lax.all_to_all(partial, ("zl", "x"), 0, 0, tiled=True)
    return pl.pallas_call(
        finish_kernel,
        out_shape=jax.ShapeDtypeStruct((X, 2 * FINE, CB * CB), jnp.float32),
        in_specs=[VMEM],
        out_specs=VMEM,
        scratch_shapes=[
            pltpu.VMEM((4 * CB, LANES), jnp.float32),
            pltpu.VMEM((FINE * 8, LANES), jnp.float32),
        ],
        compiler_params=pltpu.CompilerParams(vmem_limit_bytes=4 * MIB),
        name="finish",
    )(got)


def solution(mesh):
    devices = mesh.devices.reshape(Y, ZH, CORE, ZL, X)
    spread = Mesh(devices, AXES)
    pair, tm = ("y", "zh", "core"), ("zl", "x")
    return jax.shard_map(
        body,
        mesh=spread,
        in_specs=(P(pair, tm), P(), P(), P()),
        out_specs=P(pair, tm, None),
        check_vma=False,
    )
```

```python
import math

import jax
import jax.numpy as jnp
from jax import lax
from jax.experimental import pallas as pl
from jax.experimental.pallas import tpu as pltpu
from jax.sharding import Mesh
from jax.sharding import PartitionSpec as P

CB = 32
LAG = 128
LANES = 128
Y, ZH, CORE, ZL, X = 4, 4, 2, 4, 4
AXES = ("y", "zh", "core", "zl", "x")
PAIRS = Y * ZH * CORE
TMS = ZL * X
EIGHTHS = Y * CORE
CHUNKS = X * EIGHTHS
FINE = 8
MEDIUM = LANES // FINE
EXTRA = 8
ROWS = 2 * CB + EXTRA
MIB = 1 << 20

VMEM = pl.BlockSpec(memory_space=pltpu.VMEM)
SMEM = pl.BlockSpec(memory_space=pltpu.SMEM)
HBM = pl.BlockSpec(memory_space=pltpu.HBM)


def split_kernel(x_ref, out_ref, extra_ref):
    rows, length = x_ref.shape
    mean = jnp.sum(x_ref[...], axis=1, keepdims=True) / length
    spread = jnp.zeros((rows, 1), jnp.float32)
    for part in range(EIGHTHS):
        piece = x_ref[:, part * LANES : (part + 1) * LANES] - mean
        spread = spread + jnp.sum(piece * piece, axis=1, keepdims=True)
        out_ref[part] = piece.astype(jnp.bfloat16)
    lane = lax.broadcasted_iota(jnp.int32, (rows, LANES), 1)
    columns = jnp.where(lane == 0, mean, jnp.where(lane == 1, spread, 0.0))
    turned = jnp.transpose(jnp.concatenate([columns] * (LANES // rows), axis=0))
    wide = lax.broadcasted_iota(jnp.int32, (1, LANES), 1)
    line = jnp.where(wide < rows, turned[0:1], turned[1:2])
    high = line.astype(jnp.bfloat16).astype(jnp.float32)
    middle = (line - high).astype(jnp.bfloat16).astype(jnp.float32)
    low = line - high - middle
    row = lax.broadcasted_iota(jnp.int32, (EXTRA, LANES), 0) % (EXTRA // 2)
    lines = jnp.where(row == 0, high, jnp.where(row == 1, middle, jnp.where(row == 2, low, 0.0)))
    extra_ref[...] = lines.astype(jnp.bfloat16)


def select_kernel(rows_ref, offsets_ref, table_ref, out_ref):
    zh = lax.axis_index("zh")
    here = lax.axis_index("y") * CORE + lax.axis_index("core")
    bulk = EIGHTHS * 2 * CB
    row = lax.broadcasted_iota(jnp.int32, (EXTRA, LANES), 0)

    def fetch(block):
        block = jnp.clip(block, 0, 2 * PAIRS - 1)
        place = ((block >> 4) << 1) | ((block >> 1) & 1)
        column = (block >> 2) & (ZH - 1)
        start = pl.multiple_of(((place << 1) | (block & 1)) * CB, CB)
        data = table_ref[column, pl.ds(start, CB)]
        lines = table_ref[column, bulk:]
        lines = jnp.where(place == here, lines, jnp.zeros_like(lines))
        return data, lines

    for index in range(CHUNKS):
        place = index // X
        pair = ((place // CORE * ZH + zh) * CORE) + place % CORE
        tile = pair * X + index % X
        first = rows_ref[tile]
        data, lines = fetch(first)
        data_second, lines_second = fetch(first + offsets_ref[tile])
        out_ref[index, :CB] = data
        out_ref[index, CB : 2 * CB] = data_second
        out_ref[index, 2 * CB :] = jnp.where(row < EXTRA // 2, lines, lines_second)


def chunk_place(chunk):
    return chunk % EIGHTHS * X + chunk // EIGHTHS


def scales(edge_ref, first_half, second_half, zl, length):
    row = lax.broadcasted_iota(jnp.int32, (EXTRA, LANES), 0)
    other = jnp.where(row < EXTRA // 2, first_half, second_half) > 0
    blocks = []
    for part in range(TMS):
        start = 2 * CB + part % X * EXTRA
        parts = edge_ref[part // X, start : start + EXTRA].astype(jnp.float32)
        whole = parts + (pltpu.roll(parts, EXTRA - 1, axis=0) + pltpu.roll(parts, EXTRA - 2, axis=0))
        blocks.append(jnp.where(other, pltpu.roll(whole, LANES - CB, axis=1), whole))
    average = sum(blocks[1:], blocks[0]) / TMS
    squares = pltpu.roll(average, LANES // 2, axis=1)
    apart = [block - average for block in blocks]
    spread = [piece * piece for piece in apart]
    power = squares / length + sum(spread[1:], spread[0]) / TMS
    scaling = lax.rsqrt(power + 1e-05)

    def wanted(places):
        piece = apart[places[0]]
        for zone in range(1, ZL):
            piece = jnp.where(zl == zone, apart[places[zone]], piece)
        return piece

    columns = [scaling, wanted([max(zone * X - 1, 0) for zone in range(ZL)])]
    columns += [wanted([zone * X + x for zone in range(ZL)]) for x in range(X)]
    columns.append(wanted([min(zone * X + X, TMS - 1) for zone in range(ZL)]))
    lane = lax.broadcasted_iota(jnp.int32, (EXTRA, LANES), 1)
    turned = []
    for base in (0, EXTRA // 2):
        packed = jnp.zeros((EXTRA, LANES), jnp.float32)
        for place, column in enumerate(columns):
            packed = jnp.where(row == place, column[base : base + 1], packed)
        turned.append(jnp.where(lane < CB, packed, 0.0))
    filler = jnp.zeros((LANES - 2 * EXTRA, LANES), jnp.float32)
    turned = jnp.transpose(jnp.concatenate(turned + [filler], axis=0))
    return turned[:CB, :EXTRA], turned[:CB, EXTRA : 2 * EXTRA]


def lag_kernel(length, rows_ref, offsets_ref, live_ref, data_ref, edge_ref, out_ref, wide_a, wide_b):
    zl = lax.axis_index("zl")
    pair = (lax.axis_index("y") * ZH + lax.axis_index("zh")) * CORE + lax.axis_index("core")
    tile = pair * X + lax.axis_index("x")
    alive = live_ref[tile]
    first_half = lax.rem(rows_ref[tile], 2)
    second_half = lax.rem(rows_ref[tile] + offsets_ref[tile] + PAIRS * 2, 2)
    width = (CHUNKS + 1) * LANES
    factor = 1.0 / math.sqrt(length * TMS)

    @pl.when(alive <= 0)
    def _():
        out_ref[...] = jnp.zeros_like(out_ref)

    @pl.when(alive > 0)
    def _():
        lane = lax.broadcasted_iota(jnp.int32, (CB, LANES), 1)
        zero = jnp.zeros((CB, LANES), jnp.bfloat16)
        first_scale, second_scale = scales(edge_ref, first_half, second_half, zl, length)

        def white(piece, scale, column):
            shifted = piece.astype(jnp.float32) + scale[:, column + 2 : column + 3]
            return (shifted * scale[:, 0:1]).astype(jnp.bfloat16)

        def first_chunk(chunk):
            return white(data_ref[chunk_place(chunk), :CB], first_scale, chunk // EIGHTHS)

        def second_chunk(chunk):
            if chunk < 0:
                piece = white(edge_ref[jnp.maximum(zl - 1, 0), CB : 2 * CB], second_scale, -1)
                return jnp.where(zl > 0, piece, zero)
            if chunk >= CHUNKS:
                piece = white(edge_ref[jnp.minimum(zl + 1, ZL - 1), :CB], second_scale, X)
                return jnp.where(zl < ZL - 1, piece, zero)
            return white(data_ref[chunk_place(chunk), CB : 2 * CB], second_scale, chunk // EIGHTHS)

        here = zero
        for chunk in range(CHUNKS + 1):
            past = here
            here = first_chunk(chunk) if chunk < CHUNKS else zero
            for step in range(MEDIUM):
                shift = step * FINE
                mixed = jnp.where(lane < LANES - shift, here, past)
                turned = pltpu.roll(mixed, shift, axis=1) if shift else here
                wide_a[step * CB : (step + 1) * CB, chunk * LANES : (chunk + 1) * LANES] = turned
        later = second_chunk(-1)
        for chunk in range(-1, CHUNKS + 1):
            here = later
            later = second_chunk(chunk + 1) if chunk < CHUNKS else zero
            for step in range(FINE):
                mixed = jnp.where(lane >= step, here, later)
                turned = pltpu.roll(mixed, LANES - step, axis=1) if step else here
                wide_b[
                    step * CB : (step + 1) * CB, (chunk + 1) * LANES : (chunk + 2) * LANES
                ] = turned
        for half in range(2):
            result = lax.dot_general(
                wide_a[...],
                wide_b[:, half * LANES : half * LANES + width],
                (((1,), (1,)), ((), ())),
                preferred_element_type=jnp.float32,
            )
            rounded = (result * factor).astype(jnp.bfloat16)
            for part in range(TMS // 2):
                out_ref[half * (TMS // 2) + part] = rounded[part * 2 * CB : (part + 1) * 2 * CB]


def finish_kernel(got_ref, out_hbm, out_ref, grid_ref, turn_ref, sems):
    lane = lax.broadcasted_iota(jnp.int32, (8, LANES), 1)
    copies = []
    for slot in range(X):
        total = got_ref[slot].astype(jnp.float32)
        for zl in range(1, ZL):
            total = total + got_ref[zl * X + slot].astype(jnp.float32)
        for g in range(2):
            grid_ref[g * 2 * CB : (g + 1) * 2 * CB] = total[:, g * LANES : (g + 1) * LANES]
        for half in range(2):
            parts = [
                [
                    grid_ref[pl.ds((2 * g + half) * CB + r, 8, stride=4), :]
                    for g in range(2)
                ]
                for r in range(4)
            ]
            for q in range(FINE):
                line = None
                for r in range(4):
                    piece = parts[r][q // 4]
                    shift = (CB * (r - q % 4)) % LANES
                    piece = pltpu.roll(piece, shift, axis=1) if shift else piece
                    line = piece if line is None else jnp.where(lane >= r * CB, piece, line)
                turn_ref[q * 8 : (q + 1) * 8, :] = line
            for k in range(8):
                out_ref[slot, half * 8 : half * 8 + 8, k * LANES : (k + 1) * LANES] = turn_ref[
                    pl.ds(k, 8, stride=8), :
                ]
        copies.append(pltpu.make_async_copy(out_ref.at[slot], out_hbm.at[slot], sems.at[slot]))
        copies[-1].start()
    for copy in copies:
        copy.wait()


def body(samples, tile_rows, tile_offsets, tile_live):
    length = samples.shape[1]
    bf16 = jnp.bfloat16
    parts, lines = pl.pallas_call(
        split_kernel,
        out_shape=(
            jax.ShapeDtypeStruct((EIGHTHS, 2 * CB, LANES), bf16),
            jax.ShapeDtypeStruct((EXTRA, LANES), bf16),
        ),
        in_specs=[VMEM],
        out_specs=(VMEM, VMEM),
        compiler_params=pltpu.CompilerParams(vmem_limit_bytes=3 * MIB),
        name="split",
    )(samples)
    with jax.named_scope("spread_y"):
        table = lax.all_to_all(parts, ("y", "core"), 0, 0, tiled=True)
    with jax.named_scope("spread_z"):
        table = jnp.concatenate([table.reshape(EIGHTHS * 2 * CB, LANES), lines])
        table = lax.all_gather(table, "zh")
    chosen = pl.pallas_call(
        select_kernel,
        out_shape=jax.ShapeDtypeStruct((CHUNKS, ROWS, LANES), bf16),
        in_specs=[SMEM, SMEM, VMEM],
        out_specs=VMEM,
        compiler_params=pltpu.CompilerParams(vmem_limit_bytes=6 * MIB),
        name="select",
    )(tile_rows, tile_offsets, table)
    with jax.named_scope("collect"):
        data = lax.all_to_all(chosen, ("y", "core", "x"), 0, 0, tiled=True)
    with jax.named_scope("edges"):
        sums = jnp.sum(data[:, 2 * CB :].reshape(EIGHTHS, X * EXTRA, LANES), axis=0)
        edges = jnp.concatenate(
            [data[chunk_place(0), CB : 2 * CB], data[chunk_place(CHUNKS - 1), CB : 2 * CB], sums]
        )
        edges = lax.all_to_all(
            jnp.broadcast_to(edges[None], (ZL,) + edges.shape), "zl", 0, 0, tiled=True
        )
    partial = pl.pallas_call(
        lambda *refs: lag_kernel(length, *refs),
        out_shape=jax.ShapeDtypeStruct((TMS, 2 * CB, FINE * CB), bf16),
        in_specs=[SMEM, SMEM, SMEM, VMEM, VMEM],
        out_specs=VMEM,
        scratch_shapes=[
            pltpu.VMEM((MEDIUM * CB, (CHUNKS + 1) * LANES), bf16),
            pltpu.VMEM((FINE * CB, (CHUNKS + 2) * LANES), bf16),
        ],
        compiler_params=pltpu.CompilerParams(vmem_limit_bytes=16 * MIB),
        name="lags",
    )(tile_rows, tile_offsets, tile_live, data, edges)
    with jax.named_scope("reduce"):
        got = lax.all_to_all(partial, ("zl", "x"), 0, 0, tiled=True)
    return pl.pallas_call(
        finish_kernel,
        out_shape=jax.ShapeDtypeStruct((X, 2 * FINE, CB * CB), jnp.float32),
        in_specs=[VMEM],
        out_specs=HBM,
        scratch_shapes=[
            pltpu.VMEM((X, 2 * FINE, CB * CB), jnp.float32),
            pltpu.VMEM((4 * CB, LANES), jnp.float32),
            pltpu.VMEM((FINE * 8, LANES), jnp.float32),
            pltpu.SemaphoreType.DMA((X,)),
        ],
        compiler_params=pltpu.CompilerParams(vmem_limit_bytes=4 * MIB),
        name="finish",
    )(got)


def solution(mesh):
    devices = mesh.devices.reshape(Y, ZH, CORE, ZL, X)
    spread = Mesh(devices, AXES)
    pair, tm = ("y", "zh", "core"), ("zl", "x")
    return jax.shard_map(
        body,
        mesh=spread,
        in_specs=(P(pair, tm), P(), P(), P()),
        out_specs=P(pair, tm, None),
        check_vma=False,
    )
```

```python
import math

import jax
import jax.numpy as jnp
from jax import lax
from jax.experimental import pallas as pl
from jax.experimental.pallas import tpu as pltpu
from jax.sharding import Mesh
from jax.sharding import PartitionSpec as P

CB = 32
LAG = 128
LANES = 128
Y, ZH, CORE, ZL, X = 4, 4, 2, 4, 4
AXES = ("y", "zh", "core", "zl", "x")
PAIRS = Y * ZH * CORE
TMS = ZL * X
EIGHTHS = Y * CORE
CHUNKS = X * EIGHTHS
FINE = 8
MEDIUM = LANES // FINE
EXTRA = 8
ROWS = 2 * CB + EXTRA
MIB = 1 << 20

VMEM = pl.BlockSpec(memory_space=pltpu.VMEM)
SMEM = pl.BlockSpec(memory_space=pltpu.SMEM)
HBM = pl.BlockSpec(memory_space=pltpu.HBM)


def split_kernel(x_hbm, rows_hbm, offsets_hbm, live_hbm, out_ref, extra_ref, plan_ref, x_ref, sems):
    rows, length = x_ref.shape
    copies = [pltpu.make_async_copy(x_hbm, x_ref, sems.at[0])]
    for place, ref in enumerate((rows_hbm, offsets_hbm, live_hbm)):
        copies.append(pltpu.make_async_copy(ref, plan_ref.at[place], sems.at[place + 1]))
    for copy in copies:
        copy.start()
    copies[0].wait()
    mean = jnp.sum(x_ref[...], axis=1, keepdims=True) / length
    spread = jnp.zeros((rows, 1), jnp.float32)
    for part in range(EIGHTHS):
        piece = x_ref[:, part * LANES : (part + 1) * LANES] - mean
        spread = spread + jnp.sum(piece * piece, axis=1, keepdims=True)
        out_ref[part] = piece.astype(jnp.bfloat16)
    lane = lax.broadcasted_iota(jnp.int32, (rows, LANES), 1)
    columns = jnp.where(lane == 0, mean, jnp.where(lane == 1, spread, 0.0))
    turned = jnp.transpose(jnp.concatenate([columns] * (LANES // rows), axis=0))
    wide = lax.broadcasted_iota(jnp.int32, (1, LANES), 1)
    line = jnp.where(wide < rows, turned[0:1], turned[1:2])
    high = line.astype(jnp.bfloat16).astype(jnp.float32)
    middle = (line - high).astype(jnp.bfloat16).astype(jnp.float32)
    low = line - high - middle
    row = lax.broadcasted_iota(jnp.int32, (EXTRA, LANES), 0) % (EXTRA // 2)
    lines = jnp.where(row == 0, high, jnp.where(row == 1, middle, jnp.where(row == 2, low, 0.0)))
    extra_ref[...] = lines.astype(jnp.bfloat16)
    for copy in copies[1:]:
        copy.wait()


def select_kernel(plan_ref, table_ref, out_ref):
    zh = lax.axis_index("zh")
    here = lax.axis_index("y") * CORE + lax.axis_index("core")
    bulk = EIGHTHS * 2 * CB
    row = lax.broadcasted_iota(jnp.int32, (EXTRA, LANES), 0)

    def fetch(block):
        block = jnp.clip(block, 0, 2 * PAIRS - 1)
        place = ((block >> 4) << 1) | ((block >> 1) & 1)
        column = (block >> 2) & (ZH - 1)
        start = pl.multiple_of(((place << 1) | (block & 1)) * CB, CB)
        data = table_ref[column, pl.ds(start, CB)]
        lines = table_ref[column, bulk:]
        lines = jnp.where(place == here, lines, jnp.zeros_like(lines))
        return data, lines

    for index in range(CHUNKS):
        place = index // X
        pair = ((place // CORE * ZH + zh) * CORE) + place % CORE
        tile = pair * X + index % X
        first = plan_ref[0, 0, tile]
        data, lines = fetch(first)
        data_second, lines_second = fetch(first + plan_ref[1, 0, tile])
        out_ref[index, :CB] = data
        out_ref[index, CB : 2 * CB] = data_second
        out_ref[index, 2 * CB :] = jnp.where(row < EXTRA // 2, lines, lines_second)


def chunk_place(chunk):
    return chunk % EIGHTHS * X + chunk // EIGHTHS


def scales(edge_ref, first_half, second_half, zl, length):
    row = lax.broadcasted_iota(jnp.int32, (EXTRA, LANES), 0)
    other = jnp.where(row < EXTRA // 2, first_half, second_half) > 0
    blocks = []
    for part in range(TMS):
        start = 2 * CB + part % X * EXTRA
        parts = edge_ref[part // X, start : start + EXTRA].astype(jnp.float32)
        whole = parts + (pltpu.roll(parts, EXTRA - 1, axis=0) + pltpu.roll(parts, EXTRA - 2, axis=0))
        blocks.append(jnp.where(other, pltpu.roll(whole, LANES - CB, axis=1), whole))
    average = sum(blocks[1:], blocks[0]) / TMS
    squares = pltpu.roll(average, LANES // 2, axis=1)
    apart = [block - average for block in blocks]
    spread = [piece * piece for piece in apart]
    power = squares / length + sum(spread[1:], spread[0]) / TMS
    scaling = lax.rsqrt(power + 1e-05)

    def wanted(places):
        piece = apart[places[0]]
        for zone in range(1, ZL):
            piece = jnp.where(zl == zone, apart[places[zone]], piece)
        return piece

    columns = [scaling, wanted([max(zone * X - 1, 0) for zone in range(ZL)])]
    columns += [wanted([zone * X + x for zone in range(ZL)]) for x in range(X)]
    columns.append(wanted([min(zone * X + X, TMS - 1) for zone in range(ZL)]))
    lane = lax.broadcasted_iota(jnp.int32, (EXTRA, LANES), 1)
    turned = []
    for base in (0, EXTRA // 2):
        packed = jnp.zeros((EXTRA, LANES), jnp.float32)
        for place, column in enumerate(columns):
            packed = jnp.where(row == place, column[base : base + 1], packed)
        turned.append(jnp.where(lane < CB, packed, 0.0))
    filler = jnp.zeros((LANES - 2 * EXTRA, LANES), jnp.float32)
    turned = jnp.transpose(jnp.concatenate(turned + [filler], axis=0))
    return turned[:CB, :EXTRA], turned[:CB, EXTRA : 2 * EXTRA]


def lag_kernel(length, plan_ref, data_ref, edge_ref, out_ref, wide_a, wide_b):
    zl = lax.axis_index("zl")
    pair = (lax.axis_index("y") * ZH + lax.axis_index("zh")) * CORE + lax.axis_index("core")
    tile = pair * X + lax.axis_index("x")
    alive = plan_ref[2, 0, tile]
    first_half = plan_ref[0, 0, tile] & 1
    second_half = (plan_ref[0, 0, tile] + plan_ref[1, 0, tile]) & 1
    width = (CHUNKS + 1) * LANES
    factor = 1.0 / math.sqrt(length * TMS)

    @pl.when(alive <= 0)
    def _():
        out_ref[...] = jnp.zeros_like(out_ref)

    @pl.when(alive > 0)
    def _():
        lane = lax.broadcasted_iota(jnp.int32, (CB, LANES), 1)
        zero = jnp.zeros((CB, LANES), jnp.bfloat16)
        first_scale, second_scale = scales(edge_ref, first_half, second_half, zl, length)

        def white(piece, scale, column):
            shifted = piece.astype(jnp.float32) + scale[:, column + 2 : column + 3]
            return (shifted * scale[:, 0:1]).astype(jnp.bfloat16)

        def first_chunk(chunk):
            return white(data_ref[chunk_place(chunk), :CB], first_scale, chunk // EIGHTHS)

        def second_chunk(chunk):
            if chunk < 0:
                piece = white(edge_ref[jnp.maximum(zl - 1, 0), CB : 2 * CB], second_scale, -1)
                return jnp.where(zl > 0, piece, zero)
            if chunk >= CHUNKS:
                piece = white(edge_ref[jnp.minimum(zl + 1, ZL - 1), :CB], second_scale, X)
                return jnp.where(zl < ZL - 1, piece, zero)
            return white(data_ref[chunk_place(chunk), CB : 2 * CB], second_scale, chunk // EIGHTHS)

        here = zero
        for chunk in range(CHUNKS + 1):
            past = here
            here = first_chunk(chunk) if chunk < CHUNKS else zero
            for step in range(MEDIUM):
                shift = step * FINE
                mixed = jnp.where(lane < LANES - shift, here, past)
                turned = pltpu.roll(mixed, shift, axis=1) if shift else here
                wide_a[step * CB : (step + 1) * CB, chunk * LANES : (chunk + 1) * LANES] = turned
        later = second_chunk(-1)
        for chunk in range(-1, CHUNKS + 1):
            here = later
            later = second_chunk(chunk + 1) if chunk < CHUNKS else zero
            for step in range(FINE):
                mixed = jnp.where(lane >= step, here, later)
                turned = pltpu.roll(mixed, LANES - step, axis=1) if step else here
                wide_b[
                    step * CB : (step + 1) * CB, (chunk + 1) * LANES : (chunk + 2) * LANES
                ] = turned
        for half in range(2):
            result = lax.dot_general(
                wide_a[...],
                wide_b[:, half * LANES : half * LANES + width],
                (((1,), (1,)), ((), ())),
                preferred_element_type=jnp.float32,
            )
            rounded = (result * factor).astype(jnp.bfloat16)
            for part in range(TMS // 2):
                out_ref[half * (TMS // 2) + part] = rounded[part * 2 * CB : (part + 1) * 2 * CB]


def finish_kernel(got_ref, out_hbm, out_ref, grid_ref, turn_ref, sems):
    lane = lax.broadcasted_iota(jnp.int32, (8, LANES), 1)
    copies = []
    for slot in range(X):
        total = got_ref[slot].astype(jnp.float32)
        for zl in range(1, ZL):
            total = total + got_ref[zl * X + slot].astype(jnp.float32)
        for g in range(2):
            grid_ref[g * 2 * CB : (g + 1) * 2 * CB] = total[:, g * LANES : (g + 1) * LANES]
        for half in range(2):
            parts = [
                [
                    grid_ref[pl.ds((2 * g + half) * CB + r, 8, stride=4), :]
                    for g in range(2)
                ]
                for r in range(4)
            ]
            for q in range(FINE):
                line = None
                for r in range(4):
                    piece = parts[r][q // 4]
                    shift = (CB * (r - q % 4)) % LANES
                    piece = pltpu.roll(piece, shift, axis=1) if shift else piece
                    line = piece if line is None else jnp.where(lane >= r * CB, piece, line)
                turn_ref[q * 8 : (q + 1) * 8, :] = line
            for k in range(8):
                out_ref[slot, half * 8 : half * 8 + 8, k * LANES : (k + 1) * LANES] = turn_ref[
                    pl.ds(k, 8, stride=8), :
                ]
        copies.append(pltpu.make_async_copy(out_ref.at[slot], out_hbm.at[slot], sems.at[slot]))
        copies[-1].start()
    for copy in copies:
        copy.wait()


def body(samples, tile_rows, tile_offsets, tile_live):
    length = samples.shape[1]
    bf16 = jnp.bfloat16
    parts, lines, plan = pl.pallas_call(
        split_kernel,
        out_shape=(
            jax.ShapeDtypeStruct((EIGHTHS, 2 * CB, LANES), bf16),
            jax.ShapeDtypeStruct((EXTRA, LANES), bf16),
            jax.ShapeDtypeStruct((3, 1, LANES), jnp.int32),
        ),
        in_specs=[HBM] * 4,
        out_specs=(VMEM, VMEM, VMEM),
        scratch_shapes=[
            pltpu.VMEM(samples.shape, jnp.float32),
            pltpu.SemaphoreType.DMA((4,)),
        ],
        compiler_params=pltpu.CompilerParams(vmem_limit_bytes=3 * MIB),
        name="split",
    )(
        *(
            pltpu.with_memory_space_constraint(array, pltpu.HBM)
            for array in (samples, tile_rows[None], tile_offsets[None], tile_live[None])
        )
    )
    with jax.named_scope("spread_y"):
        table = lax.all_to_all(parts, ("y", "core"), 0, 0, tiled=True)
    with jax.named_scope("spread_z"):
        table = jnp.concatenate([table.reshape(EIGHTHS * 2 * CB, LANES), lines])
        table = lax.all_gather(table, "zh")
    chosen = pl.pallas_call(
        select_kernel,
        out_shape=jax.ShapeDtypeStruct((CHUNKS, ROWS, LANES), bf16),
        in_specs=[SMEM, VMEM],
        out_specs=VMEM,
        compiler_params=pltpu.CompilerParams(vmem_limit_bytes=6 * MIB),
        name="select",
    )(plan, table)
    with jax.named_scope("collect"):
        data = lax.all_to_all(chosen, ("y", "core", "x"), 0, 0, tiled=True)
    with jax.named_scope("edges"):
        sums = jnp.sum(data[:, 2 * CB :].reshape(EIGHTHS, X * EXTRA, LANES), axis=0)
        edges = jnp.concatenate(
            [data[chunk_place(0), CB : 2 * CB], data[chunk_place(CHUNKS - 1), CB : 2 * CB], sums]
        )
        edges = lax.all_to_all(
            jnp.broadcast_to(edges[None], (ZL,) + edges.shape), "zl", 0, 0, tiled=True
        )
    partial = pl.pallas_call(
        lambda *refs: lag_kernel(length, *refs),
        out_shape=jax.ShapeDtypeStruct((TMS, 2 * CB, FINE * CB), bf16),
        in_specs=[SMEM, VMEM, VMEM],
        out_specs=VMEM,
        scratch_shapes=[
            pltpu.VMEM((MEDIUM * CB, (CHUNKS + 1) * LANES), bf16),
            pltpu.VMEM((FINE * CB, (CHUNKS + 2) * LANES), bf16),
        ],
        compiler_params=pltpu.CompilerParams(vmem_limit_bytes=16 * MIB),
        name="lags",
    )(plan, data, edges)
    with jax.named_scope("reduce"):
        got = lax.all_to_all(partial, ("zl", "x"), 0, 0, tiled=True)
    return pl.pallas_call(
        finish_kernel,
        out_shape=jax.ShapeDtypeStruct((X, 2 * FINE, CB * CB), jnp.float32),
        in_specs=[VMEM],
        out_specs=HBM,
        scratch_shapes=[
            pltpu.VMEM((X, 2 * FINE, CB * CB), jnp.float32),
            pltpu.VMEM((4 * CB, LANES), jnp.float32),
            pltpu.VMEM((FINE * 8, LANES), jnp.float32),
            pltpu.SemaphoreType.DMA((X,)),
        ],
        compiler_params=pltpu.CompilerParams(vmem_limit_bytes=4 * MIB),
        name="finish",
    )(got)


def solution(mesh):
    devices = mesh.devices.reshape(Y, ZH, CORE, ZL, X)
    spread = Mesh(devices, AXES)
    pair, tm = ("y", "zh", "core"), ("zl", "x")
    return jax.shard_map(
        body,
        mesh=spread,
        in_specs=(P(pair, tm), P(), P(), P()),
        out_specs=P(pair, tm, None),
        check_vma=False,
    )
```

```python
import math

import jax
import jax.numpy as jnp
from jax import lax
from jax.experimental import pallas as pl
from jax.experimental.pallas import tpu as pltpu
from jax.sharding import Mesh
from jax.sharding import PartitionSpec as P

CB = 32
LAG = 128
LANES = 128
Y, ZH, CORE, ZL, X = 4, 4, 2, 4, 4
AXES = ("y", "zh", "core", "zl", "x")
PAIRS = Y * ZH * CORE
TMS = ZL * X
EIGHTHS = Y * CORE
CHUNKS = X * EIGHTHS
FINE = 8
MEDIUM = LANES // FINE
EXTRA = 8
ROWS = 2 * CB + EXTRA
MIB = 1 << 20

VMEM = pl.BlockSpec(memory_space=pltpu.VMEM)
SMEM = pl.BlockSpec(memory_space=pltpu.SMEM)
HBM = pl.BlockSpec(memory_space=pltpu.HBM)


def split_kernel(x_hbm, rows_hbm, offsets_hbm, live_hbm, out_ref, extra_ref, plan_ref, x_ref, sems):
    rows, length = x_ref.shape
    copies = [pltpu.make_async_copy(x_hbm, x_ref, sems.at[0])]
    for place, ref in enumerate((rows_hbm, offsets_hbm, live_hbm)):
        copies.append(pltpu.make_async_copy(ref, plan_ref.at[place], sems.at[place + 1]))
    for copy in copies:
        copy.start()
    copies[0].wait()
    mean = jnp.sum(x_ref[...], axis=1, keepdims=True) / length
    spread = jnp.zeros((rows, 1), jnp.float32)
    for part in range(EIGHTHS):
        piece = x_ref[:, part * LANES : (part + 1) * LANES] - mean
        spread = spread + jnp.sum(piece * piece, axis=1, keepdims=True)
        out_ref[part] = piece.astype(jnp.bfloat16)
    lane = lax.broadcasted_iota(jnp.int32, (rows, LANES), 1)
    columns = jnp.where(lane == 0, mean, jnp.where(lane == 1, spread, 0.0))
    turned = jnp.transpose(jnp.concatenate([columns] * (LANES // rows), axis=0))
    wide = lax.broadcasted_iota(jnp.int32, (1, LANES), 1)
    line = jnp.where(wide < rows, turned[0:1], turned[1:2])
    high = line.astype(jnp.bfloat16).astype(jnp.float32)
    middle = (line - high).astype(jnp.bfloat16).astype(jnp.float32)
    low = line - high - middle
    row = lax.broadcasted_iota(jnp.int32, (EXTRA, LANES), 0) % (EXTRA // 2)
    lines = jnp.where(row == 0, high, jnp.where(row == 1, middle, jnp.where(row == 2, low, 0.0)))
    extra_ref[...] = lines.astype(jnp.bfloat16)
    for copy in copies[1:]:
        copy.wait()


def select_kernel(plan_ref, table_ref, out_ref):
    zh = lax.axis_index("zh")
    here = lax.axis_index("y") * CORE + lax.axis_index("core")
    bulk = EIGHTHS * 2 * CB
    row = lax.broadcasted_iota(jnp.int32, (EXTRA, LANES), 0)

    def fetch(block):
        block = jnp.clip(block, 0, 2 * PAIRS - 1)
        place = ((block >> 4) << 1) | ((block >> 1) & 1)
        column = (block >> 2) & (ZH - 1)
        start = pl.multiple_of(((place << 1) | (block & 1)) * CB, CB)
        data = table_ref[column, pl.ds(start, CB)]
        lines = table_ref[column, bulk:]
        lines = jnp.where(place == here, lines, jnp.zeros_like(lines))
        return data, lines

    for index in range(CHUNKS):
        place = index // X
        pair = ((place // CORE * ZH + zh) * CORE) + place % CORE
        tile = pair * X + index % X
        first = plan_ref[0, 0, tile]
        data, lines = fetch(first)
        data_second, lines_second = fetch(first + plan_ref[1, 0, tile])
        out_ref[index, :CB] = data
        out_ref[index, CB : 2 * CB] = data_second
        out_ref[index, 2 * CB :] = jnp.where(row < EXTRA // 2, lines, lines_second)


def chunk_place(chunk):
    return chunk % EIGHTHS * X + chunk // EIGHTHS


def scales(edge_ref, first_half, second_half, zl, length):
    row = lax.broadcasted_iota(jnp.int32, (EXTRA, LANES), 0)
    other = jnp.where(row < EXTRA // 2, first_half, second_half) > 0
    blocks = []
    for part in range(TMS):
        start = 2 * CB + part % X * EXTRA
        parts = edge_ref[part // X, start : start + EXTRA].astype(jnp.float32)
        whole = parts + (pltpu.roll(parts, EXTRA - 1, axis=0) + pltpu.roll(parts, EXTRA - 2, axis=0))
        blocks.append(jnp.where(other, pltpu.roll(whole, LANES - CB, axis=1), whole))
    average = sum(blocks[1:], blocks[0]) / TMS
    squares = pltpu.roll(average, LANES // 2, axis=1)
    apart = [block - average for block in blocks]
    spread = [piece * piece for piece in apart]
    power = squares / length + sum(spread[1:], spread[0]) / TMS
    scaling = lax.rsqrt(power + 1e-05)

    def wanted(places):
        piece = apart[places[0]]
        for zone in range(1, ZL):
            piece = jnp.where(zl == zone, apart[places[zone]], piece)
        return piece

    columns = [scaling, wanted([max(zone * X - 1, 0) for zone in range(ZL)])]
    columns += [wanted([zone * X + x for zone in range(ZL)]) for x in range(X)]
    columns.append(wanted([min(zone * X + X, TMS - 1) for zone in range(ZL)]))
    lane = lax.broadcasted_iota(jnp.int32, (EXTRA, LANES), 1)
    turned = []
    for base in (0, EXTRA // 2):
        packed = jnp.zeros((EXTRA, LANES), jnp.float32)
        for place, column in enumerate(columns):
            packed = jnp.where(row == place, column[base : base + 1], packed)
        turned.append(jnp.where(lane < CB, packed, 0.0))
    filler = jnp.zeros((LANES - 2 * EXTRA, LANES), jnp.float32)
    turned = jnp.transpose(jnp.concatenate(turned + [filler], axis=0))
    return turned[:CB, :EXTRA], turned[:CB, EXTRA : 2 * EXTRA]


def lag_kernel(length, plan_ref, data_ref, edge_ref, out_ref, wide_a, wide_b):
    zl = lax.axis_index("zl")
    pair = (lax.axis_index("y") * ZH + lax.axis_index("zh")) * CORE + lax.axis_index("core")
    tile = pair * X + lax.axis_index("x")
    alive = plan_ref[2, 0, tile]
    first_half = plan_ref[0, 0, tile] & 1
    second_half = (plan_ref[0, 0, tile] + plan_ref[1, 0, tile]) & 1
    width = (CHUNKS + 1) * LANES
    factor = 1.0 / math.sqrt(length * TMS)

    @pl.when(alive <= 0)
    def _():
        out_ref[...] = jnp.zeros_like(out_ref)

    @pl.when(alive > 0)
    def _():
        lane = lax.broadcasted_iota(jnp.int32, (CB, LANES), 1)
        zero = jnp.zeros((CB, LANES), jnp.bfloat16)
        first_scale, second_scale = scales(edge_ref, first_half, second_half, zl, length)

        def white(piece, scale, column):
            shifted = piece.astype(jnp.float32) + scale[:, column + 2 : column + 3]
            return (shifted * scale[:, 0:1]).astype(jnp.bfloat16)

        def first_chunk(chunk):
            return white(data_ref[chunk_place(chunk), :CB], first_scale, chunk // EIGHTHS)

        def second_chunk(chunk):
            if chunk < 0:
                piece = white(edge_ref[jnp.maximum(zl - 1, 0), CB : 2 * CB], second_scale, -1)
                return jnp.where(zl > 0, piece, zero)
            if chunk >= CHUNKS:
                piece = white(edge_ref[jnp.minimum(zl + 1, ZL - 1), :CB], second_scale, X)
                return jnp.where(zl < ZL - 1, piece, zero)
            return white(data_ref[chunk_place(chunk), CB : 2 * CB], second_scale, chunk // EIGHTHS)

        here = zero
        for chunk in range(CHUNKS + 1):
            past = here
            here = first_chunk(chunk) if chunk < CHUNKS else zero
            for step in range(MEDIUM):
                shift = step * FINE
                mixed = jnp.where(lane < LANES - shift, here, past)
                turned = pltpu.roll(mixed, shift, axis=1) if shift else here
                wide_a[step * CB : (step + 1) * CB, chunk * LANES : (chunk + 1) * LANES] = turned
        later = second_chunk(-1)
        for chunk in range(-1, CHUNKS + 1):
            here = later
            later = second_chunk(chunk + 1) if chunk < CHUNKS else zero
            for step in range(FINE):
                mixed = jnp.where(lane >= step, here, later)
                turned = pltpu.roll(mixed, LANES - step, axis=1) if step else here
                wide_b[
                    step * CB : (step + 1) * CB, (chunk + 1) * LANES : (chunk + 2) * LANES
                ] = turned
        for half in range(2):
            result = lax.dot_general(
                wide_a[...],
                wide_b[:, half * LANES : half * LANES + width],
                (((1,), (1,)), ((), ())),
                preferred_element_type=jnp.float32,
            )
            rounded = (result * factor).astype(jnp.bfloat16)
            for part in range(TMS // 2):
                out_ref[half * (TMS // 2) + part] = rounded[part * 2 * CB : (part + 1) * 2 * CB]


def finish_kernel(got_ref, out_hbm, out_ref, grid_ref, turn_ref, sems):
    lane = lax.broadcasted_iota(jnp.int32, (8, LANES), 1)
    copies = []
    for slot in range(X):
        total = got_ref[slot].astype(jnp.float32)
        for zl in range(1, ZL):
            total = total + got_ref[zl * X + slot].astype(jnp.float32)
        for g in range(2):
            grid_ref[g * 2 * CB : (g + 1) * 2 * CB] = total[:, g * LANES : (g + 1) * LANES]
        for half in range(2):
            parts = [
                [
                    grid_ref[pl.ds((2 * g + half) * CB + r, 8, stride=4), :]
                    for g in range(2)
                ]
                for r in range(4)
            ]
            for q in range(FINE):
                line = None
                for r in range(4):
                    piece = parts[r][q // 4]
                    shift = (CB * (r - q % 4)) % LANES
                    piece = pltpu.roll(piece, shift, axis=1) if shift else piece
                    line = piece if line is None else jnp.where(lane >= r * CB, piece, line)
                turn_ref[q * 8 : (q + 1) * 8, :] = line
            for k in range(8):
                out_ref[slot, half * 8 : half * 8 + 8, k * LANES : (k + 1) * LANES] = turn_ref[
                    pl.ds(k, 8, stride=8), :
                ]
        copies.append(pltpu.make_async_copy(out_ref.at[slot], out_hbm.at[slot], sems.at[slot]))
        copies[-1].start()
    for copy in copies:
        copy.wait()


def body(samples, tile_rows, tile_offsets, tile_live):
    length = samples.shape[1]
    bf16 = jnp.bfloat16
    parts, lines, plan = pl.pallas_call(
        split_kernel,
        out_shape=(
            jax.ShapeDtypeStruct((EIGHTHS, 2 * CB, LANES), bf16),
            jax.ShapeDtypeStruct((EXTRA, LANES), bf16),
            pltpu.SMEM((3, 1, LANES), jnp.int32),
        ),
        in_specs=[HBM] * 4,
        out_specs=(VMEM, VMEM, SMEM),
        scratch_shapes=[
            pltpu.VMEM(samples.shape, jnp.float32),
            pltpu.SemaphoreType.DMA((4,)),
        ],
        compiler_params=pltpu.CompilerParams(vmem_limit_bytes=3 * MIB),
        name="split",
    )(
        *(
            pltpu.with_memory_space_constraint(array, pltpu.HBM)
            for array in (samples, tile_rows[None], tile_offsets[None], tile_live[None])
        )
    )
    with jax.named_scope("spread_y"):
        table = lax.all_to_all(parts, ("y", "core"), 0, 0, tiled=True)
    with jax.named_scope("spread_z"):
        table = jnp.concatenate([table.reshape(EIGHTHS * 2 * CB, LANES), lines])
        table = lax.all_gather(table, "zh")
    chosen = pl.pallas_call(
        select_kernel,
        out_shape=jax.ShapeDtypeStruct((CHUNKS, ROWS, LANES), bf16),
        in_specs=[SMEM, VMEM],
        out_specs=VMEM,
        compiler_params=pltpu.CompilerParams(vmem_limit_bytes=6 * MIB),
        name="select",
    )(pltpu.with_memory_space_constraint(plan, pltpu.SMEM), table)
    with jax.named_scope("collect"):
        data = lax.all_to_all(chosen, ("y", "core", "x"), 0, 0, tiled=True)
    with jax.named_scope("edges"):
        sums = jnp.sum(data[:, 2 * CB :].reshape(EIGHTHS, X * EXTRA, LANES), axis=0)
        edges = jnp.concatenate(
            [data[chunk_place(0), CB : 2 * CB], data[chunk_place(CHUNKS - 1), CB : 2 * CB], sums]
        )
        edges = lax.all_to_all(
            jnp.broadcast_to(edges[None], (ZL,) + edges.shape), "zl", 0, 0, tiled=True
        )
    partial = pl.pallas_call(
        lambda *refs: lag_kernel(length, *refs),
        out_shape=jax.ShapeDtypeStruct((TMS, 2 * CB, FINE * CB), bf16),
        in_specs=[SMEM, VMEM, VMEM],
        out_specs=VMEM,
        scratch_shapes=[
            pltpu.VMEM((MEDIUM * CB, (CHUNKS + 1) * LANES), bf16),
            pltpu.VMEM((FINE * CB, (CHUNKS + 2) * LANES), bf16),
        ],
        compiler_params=pltpu.CompilerParams(vmem_limit_bytes=16 * MIB),
        name="lags",
    )(pltpu.with_memory_space_constraint(plan, pltpu.SMEM), data, edges)
    with jax.named_scope("reduce"):
        got = lax.all_to_all(partial, ("zl", "x"), 0, 0, tiled=True)
    return pl.pallas_call(
        finish_kernel,
        out_shape=jax.ShapeDtypeStruct((X, 2 * FINE, CB * CB), jnp.float32),
        in_specs=[VMEM],
        out_specs=HBM,
        scratch_shapes=[
            pltpu.VMEM((X, 2 * FINE, CB * CB), jnp.float32),
            pltpu.VMEM((4 * CB, LANES), jnp.float32),
            pltpu.VMEM((FINE * 8, LANES), jnp.float32),
            pltpu.SemaphoreType.DMA((X,)),
        ],
        compiler_params=pltpu.CompilerParams(vmem_limit_bytes=4 * MIB),
        name="finish",
    )(got)


def solution(mesh):
    devices = mesh.devices.reshape(Y, ZH, CORE, ZL, X)
    spread = Mesh(devices, AXES)
    pair, tm = ("y", "zh", "core"), ("zl", "x")
    return jax.shard_map(
        body,
        mesh=spread,
        in_specs=(P(pair, tm), P(), P(), P()),
        out_specs=P(pair, tm, None),
        check_vma=False,
    )
```

```python
import math

import jax
import jax.numpy as jnp
from jax import lax
from jax.experimental import pallas as pl
from jax.experimental.pallas import tpu as pltpu
from jax.sharding import Mesh
from jax.sharding import PartitionSpec as P

CB = 32
LAG = 128
LANES = 128
Y, ZH, CORE, ZL, X = 4, 4, 2, 4, 4
AXES = ("y", "zh", "core", "zl", "x")
PAIRS = Y * ZH * CORE
TMS = ZL * X
EIGHTHS = Y * CORE
CHUNKS = X * EIGHTHS
FINE = 8
MEDIUM = LANES // FINE
EXTRA = 8
ROWS = 2 * CB + EXTRA
MIB = 1 << 20

VMEM = pl.BlockSpec(memory_space=pltpu.VMEM)
SMEM = pl.BlockSpec(memory_space=pltpu.SMEM)
HBM = pl.BlockSpec(memory_space=pltpu.HBM)


def split_kernel(x_hbm, rows_hbm, offsets_hbm, live_hbm, out_ref, extra_ref, plan_ref, x_ref, sems):
    rows, length = x_ref.shape
    copies = [pltpu.make_async_copy(x_hbm, x_ref, sems.at[0])]
    for place, ref in enumerate((rows_hbm, offsets_hbm, live_hbm)):
        copies.append(pltpu.make_async_copy(ref, plan_ref.at[place], sems.at[place + 1]))
    for copy in copies:
        copy.start()
    copies[0].wait()
    mean = jnp.sum(x_ref[...], axis=1, keepdims=True) / length
    spread = jnp.zeros((rows, 1), jnp.float32)
    for part in range(EIGHTHS):
        piece = x_ref[:, part * LANES : (part + 1) * LANES] - mean
        spread = spread + jnp.sum(piece * piece, axis=1, keepdims=True)
        out_ref[part] = piece.astype(jnp.bfloat16)
    lane = lax.broadcasted_iota(jnp.int32, (rows, LANES), 1)
    channel = lax.broadcasted_iota(jnp.int32, (rows, LANES), 0)
    placed = jnp.where(lane == channel, mean, jnp.where(lane == channel + rows, spread, 0.0))
    line = jnp.sum(placed, axis=0, keepdims=True)
    high = line.astype(jnp.bfloat16).astype(jnp.float32)
    middle = (line - high).astype(jnp.bfloat16).astype(jnp.float32)
    low = line - high - middle
    row = lax.broadcasted_iota(jnp.int32, (EXTRA, LANES), 0) % (EXTRA // 2)
    lines = jnp.where(row == 0, high, jnp.where(row == 1, middle, jnp.where(row == 2, low, 0.0)))
    extra_ref[...] = lines.astype(jnp.bfloat16)
    for copy in copies[1:]:
        copy.wait()


def select_kernel(plan_ref, table_ref, out_ref):
    zh = lax.axis_index("zh")
    here = lax.axis_index("y") * CORE + lax.axis_index("core")
    bulk = EIGHTHS * 2 * CB
    row = lax.broadcasted_iota(jnp.int32, (EXTRA, LANES), 0)

    def fetch(block):
        block = jnp.clip(block, 0, 2 * PAIRS - 1)
        place = ((block >> 4) << 1) | ((block >> 1) & 1)
        column = (block >> 2) & (ZH - 1)
        start = pl.multiple_of(((place << 1) | (block & 1)) * CB, CB)
        data = table_ref[column, pl.ds(start, CB)]
        lines = table_ref[column, bulk:]
        lines = jnp.where(place == here, lines, jnp.zeros_like(lines))
        return data, lines

    for index in range(CHUNKS):
        place = index // X
        pair = ((place // CORE * ZH + zh) * CORE) + place % CORE
        tile = pair * X + index % X
        first = plan_ref[0, 0, tile]
        data, lines = fetch(first)
        data_second, lines_second = fetch(first + plan_ref[1, 0, tile])
        out_ref[index, :CB] = data
        out_ref[index, CB : 2 * CB] = data_second
        out_ref[index, 2 * CB :] = jnp.where(row < EXTRA // 2, lines, lines_second)


def chunk_place(chunk):
    return chunk % EIGHTHS * X + chunk // EIGHTHS


def scales(edge_ref, first_half, second_half, zl, length):
    row = lax.broadcasted_iota(jnp.int32, (EXTRA, LANES), 0)
    other = jnp.where(row < EXTRA // 2, first_half, second_half) > 0
    blocks = []
    for part in range(TMS):
        start = 2 * CB + part % X * EXTRA
        parts = edge_ref[part // X, start : start + EXTRA].astype(jnp.float32)
        whole = parts + (pltpu.roll(parts, EXTRA - 1, axis=0) + pltpu.roll(parts, EXTRA - 2, axis=0))
        blocks.append(jnp.where(other, pltpu.roll(whole, LANES - CB, axis=1), whole))
    average = sum(blocks[1:], blocks[0]) / TMS
    squares = pltpu.roll(average, LANES // 2, axis=1)
    apart = [block - average for block in blocks]
    spread = [piece * piece for piece in apart]
    power = squares / length + sum(spread[1:], spread[0]) / TMS
    scaling = lax.rsqrt(power + 1e-05)

    def wanted(places):
        piece = apart[places[0]]
        for zone in range(1, ZL):
            piece = jnp.where(zl == zone, apart[places[zone]], piece)
        return piece

    columns = [scaling, wanted([max(zone * X - 1, 0) for zone in range(ZL)])]
    columns += [wanted([zone * X + x for zone in range(ZL)]) for x in range(X)]
    columns.append(wanted([min(zone * X + X, TMS - 1) for zone in range(ZL)]))
    lane = lax.broadcasted_iota(jnp.int32, (EXTRA, LANES), 1)
    turned = []
    for base in (0, EXTRA // 2):
        packed = jnp.zeros((EXTRA, LANES), jnp.float32)
        for place, column in enumerate(columns):
            packed = jnp.where(row == place, column[base : base + 1], packed)
        turned.append(jnp.where(lane < CB, packed, 0.0))
    filler = jnp.zeros((LANES - 2 * EXTRA, LANES), jnp.float32)
    turned = jnp.transpose(jnp.concatenate(turned + [filler], axis=0))
    return turned[:CB, :EXTRA], turned[:CB, EXTRA : 2 * EXTRA]


def lag_kernel(length, plan_ref, data_ref, edge_ref, out_ref, wide_a, wide_b):
    zl = lax.axis_index("zl")
    pair = (lax.axis_index("y") * ZH + lax.axis_index("zh")) * CORE + lax.axis_index("core")
    tile = pair * X + lax.axis_index("x")
    alive = plan_ref[2, 0, tile]
    first_half = plan_ref[0, 0, tile] & 1
    second_half = (plan_ref[0, 0, tile] + plan_ref[1, 0, tile]) & 1
    width = (CHUNKS + 1) * LANES
    factor = 1.0 / math.sqrt(length * TMS)

    @pl.when(alive <= 0)
    def _():
        out_ref[...] = jnp.zeros_like(out_ref)

    @pl.when(alive > 0)
    def _():
        lane = lax.broadcasted_iota(jnp.int32, (CB, LANES), 1)
        zero = jnp.zeros((CB, LANES), jnp.bfloat16)
        first_scale, second_scale = scales(edge_ref, first_half, second_half, zl, length)

        def white(piece, scale, column):
            shifted = piece.astype(jnp.float32) + scale[:, column + 2 : column + 3]
            return (shifted * scale[:, 0:1]).astype(jnp.bfloat16)

        def first_chunk(chunk):
            return white(data_ref[chunk_place(chunk), :CB], first_scale, chunk // EIGHTHS)

        def second_chunk(chunk):
            if chunk < 0:
                piece = white(edge_ref[jnp.maximum(zl - 1, 0), CB : 2 * CB], second_scale, -1)
                return jnp.where(zl > 0, piece, zero)
            if chunk >= CHUNKS:
                piece = white(edge_ref[jnp.minimum(zl + 1, ZL - 1), :CB], second_scale, X)
                return jnp.where(zl < ZL - 1, piece, zero)
            return white(data_ref[chunk_place(chunk), CB : 2 * CB], second_scale, chunk // EIGHTHS)

        here = zero
        for chunk in range(CHUNKS + 1):
            past = here
            here = first_chunk(chunk) if chunk < CHUNKS else zero
            for step in range(MEDIUM):
                shift = step * FINE
                mixed = jnp.where(lane < LANES - shift, here, past)
                turned = pltpu.roll(mixed, shift, axis=1) if shift else here
                wide_a[step * CB : (step + 1) * CB, chunk * LANES : (chunk + 1) * LANES] = turned
        later = second_chunk(-1)
        for chunk in range(-1, CHUNKS + 1):
            here = later
            later = second_chunk(chunk + 1) if chunk < CHUNKS else zero
            for step in range(FINE):
                mixed = jnp.where(lane >= step, here, later)
                turned = pltpu.roll(mixed, LANES - step, axis=1) if step else here
                wide_b[
                    step * CB : (step + 1) * CB, (chunk + 1) * LANES : (chunk + 2) * LANES
                ] = turned
        for half in range(2):
            result = lax.dot_general(
                wide_a[...],
                wide_b[:, half * LANES : half * LANES + width],
                (((1,), (1,)), ((), ())),
                preferred_element_type=jnp.float32,
            )
            rounded = (result * factor).astype(jnp.bfloat16)
            for part in range(TMS // 2):
                out_ref[half * (TMS // 2) + part] = rounded[part * 2 * CB : (part + 1) * 2 * CB]


def finish_kernel(got_ref, out_hbm, out_ref, grid_ref, turn_ref, sem):
    lane = lax.broadcasted_iota(jnp.int32, (8, LANES), 1)
    for slot in range(X):
        total = got_ref[slot].astype(jnp.float32)
        for zl in range(1, ZL):
            total = total + got_ref[zl * X + slot].astype(jnp.float32)
        for g in range(2):
            grid_ref[g * 2 * CB : (g + 1) * 2 * CB] = total[:, g * LANES : (g + 1) * LANES]
        for half in range(2):
            parts = [
                [
                    grid_ref[pl.ds((2 * g + half) * CB + r, 8, stride=4), :]
                    for g in range(2)
                ]
                for r in range(4)
            ]
            for q in range(FINE):
                line = None
                for r in range(4):
                    piece = parts[r][q // 4]
                    shift = (CB * (r - q % 4)) % LANES
                    piece = pltpu.roll(piece, shift, axis=1) if shift else piece
                    line = piece if line is None else jnp.where(lane >= r * CB, piece, line)
                turn_ref[q * 8 : (q + 1) * 8, :] = line
            for k in range(8):
                out_ref[slot, half * 8 : half * 8 + 8, k * LANES : (k + 1) * LANES] = turn_ref[
                    pl.ds(k, 8, stride=8), :
                ]
    copy = pltpu.make_async_copy(out_ref, out_hbm, sem)
    copy.start()
    copy.wait()


def body(samples, tile_rows, tile_offsets, tile_live):
    length = samples.shape[1]
    bf16 = jnp.bfloat16
    parts, lines, plan = pl.pallas_call(
        split_kernel,
        out_shape=(
            jax.ShapeDtypeStruct((EIGHTHS, 2 * CB, LANES), bf16),
            jax.ShapeDtypeStruct((EXTRA, LANES), bf16),
            pltpu.SMEM((3, 1, LANES), jnp.int32),
        ),
        in_specs=[HBM] * 4,
        out_specs=(VMEM, VMEM, SMEM),
        scratch_shapes=[
            pltpu.VMEM(samples.shape, jnp.float32),
            pltpu.SemaphoreType.DMA((4,)),
        ],
        compiler_params=pltpu.CompilerParams(vmem_limit_bytes=3 * MIB),
        name="split",
    )(
        *(
            pltpu.with_memory_space_constraint(array, pltpu.HBM)
            for array in (samples, tile_rows[None], tile_offsets[None], tile_live[None])
        )
    )
    with jax.named_scope("spread_y"):
        table = lax.all_to_all(parts, ("y", "core"), 0, 0, tiled=True)
    with jax.named_scope("spread_z"):
        table = jnp.concatenate([table.reshape(EIGHTHS * 2 * CB, LANES), lines])
        table = lax.all_gather(table, "zh")
    chosen = pl.pallas_call(
        select_kernel,
        out_shape=jax.ShapeDtypeStruct((CHUNKS, ROWS, LANES), bf16),
        in_specs=[SMEM, VMEM],
        out_specs=VMEM,
        compiler_params=pltpu.CompilerParams(vmem_limit_bytes=6 * MIB),
        name="select",
    )(pltpu.with_memory_space_constraint(plan, pltpu.SMEM), table)
    with jax.named_scope("collect"):
        data = lax.all_to_all(chosen, ("y", "core", "x"), 0, 0, tiled=True)
    with jax.named_scope("edges"):
        sums = jnp.sum(data[:, 2 * CB :].reshape(EIGHTHS, X * EXTRA, LANES), axis=0)
        edges = jnp.concatenate(
            [data[chunk_place(0), CB : 2 * CB], data[chunk_place(CHUNKS - 1), CB : 2 * CB], sums]
        )
        edges = lax.all_to_all(
            jnp.broadcast_to(edges[None], (ZL,) + edges.shape), "zl", 0, 0, tiled=True
        )
    partial = pl.pallas_call(
        lambda *refs: lag_kernel(length, *refs),
        out_shape=jax.ShapeDtypeStruct((TMS, 2 * CB, FINE * CB), bf16),
        in_specs=[SMEM, VMEM, VMEM],
        out_specs=VMEM,
        scratch_shapes=[
            pltpu.VMEM((MEDIUM * CB, (CHUNKS + 1) * LANES), bf16),
            pltpu.VMEM((FINE * CB, (CHUNKS + 2) * LANES), bf16),
        ],
        compiler_params=pltpu.CompilerParams(vmem_limit_bytes=16 * MIB),
        name="lags",
    )(pltpu.with_memory_space_constraint(plan, pltpu.SMEM), data, edges)
    with jax.named_scope("reduce"):
        got = lax.all_to_all(partial, ("zl", "x"), 0, 0, tiled=True)
    return pl.pallas_call(
        finish_kernel,
        out_shape=jax.ShapeDtypeStruct((X, 2 * FINE, CB * CB), jnp.float32),
        in_specs=[VMEM],
        out_specs=HBM,
        scratch_shapes=[
            pltpu.VMEM((X, 2 * FINE, CB * CB), jnp.float32),
            pltpu.VMEM((4 * CB, LANES), jnp.float32),
            pltpu.VMEM((FINE * 8, LANES), jnp.float32),
            pltpu.SemaphoreType.DMA,
        ],
        compiler_params=pltpu.CompilerParams(vmem_limit_bytes=4 * MIB),
        name="finish",
    )(got)


def solution(mesh):
    devices = mesh.devices.reshape(Y, ZH, CORE, ZL, X)
    spread = Mesh(devices, AXES)
    pair, tm = ("y", "zh", "core"), ("zl", "x")
    return jax.shard_map(
        body,
        mesh=spread,
        in_specs=(P(pair, tm), P(), P(), P()),
        out_specs=P(pair, tm, None),
        check_vma=False,
    )
```

```python
import math

import jax
import jax.numpy as jnp
from jax import lax
from jax.experimental import pallas as pl
from jax.experimental.pallas import tpu as pltpu
from jax.sharding import Mesh
from jax.sharding import PartitionSpec as P

CB = 32
LAG = 128
LANES = 128
Y, ZH, CORE, ZL, X = 4, 4, 2, 4, 4
AXES = ("y", "zh", "core", "zl", "x")
PAIRS = Y * ZH * CORE
TMS = ZL * X
EIGHTHS = Y * CORE
CHUNKS = X * EIGHTHS
FINE = 8
MEDIUM = LANES // FINE
EXTRA = 8
ROWS = 2 * CB + EXTRA
MIB = 1 << 20

VMEM = pl.BlockSpec(memory_space=pltpu.VMEM)
SMEM = pl.BlockSpec(memory_space=pltpu.SMEM)
HBM = pl.BlockSpec(memory_space=pltpu.HBM)


def split_kernel(x_hbm, rows_hbm, offsets_hbm, live_hbm, out_ref, extra_ref, plan_ref, x_ref, sems):
    rows, length = x_ref.shape
    copies = [pltpu.make_async_copy(x_hbm, x_ref, sems.at[0])]
    for place, ref in enumerate((rows_hbm, offsets_hbm, live_hbm)):
        copies.append(pltpu.make_async_copy(ref, plan_ref.at[place], sems.at[place + 1]))
    for copy in copies:
        copy.start()
    copies[0].wait()
    mean = jnp.sum(x_ref[...], axis=1, keepdims=True) / length
    spread = jnp.zeros((rows, 1), jnp.float32)
    for part in range(EIGHTHS):
        piece = x_ref[:, part * LANES : (part + 1) * LANES] - mean
        spread = spread + jnp.sum(piece * piece, axis=1, keepdims=True)
        out_ref[part] = piece.astype(jnp.bfloat16)
    lane = lax.broadcasted_iota(jnp.int32, (rows, LANES), 1)
    channel = lax.broadcasted_iota(jnp.int32, (rows, LANES), 0)
    placed = jnp.where(lane == channel, mean, jnp.where(lane == channel + rows, spread, 0.0))
    line = jnp.sum(placed, axis=0, keepdims=True)
    high = line.astype(jnp.bfloat16).astype(jnp.float32)
    middle = (line - high).astype(jnp.bfloat16).astype(jnp.float32)
    low = line - high - middle
    row = lax.broadcasted_iota(jnp.int32, (EXTRA, LANES), 0) % (EXTRA // 2)
    lines = jnp.where(row == 0, high, jnp.where(row == 1, middle, jnp.where(row == 2, low, 0.0)))
    extra_ref[...] = lines.astype(jnp.bfloat16)
    for copy in copies[1:]:
        copy.wait()


def select_kernel(plan_ref, table_ref, out_ref):
    zh = lax.axis_index("zh")
    here = lax.axis_index("y") * CORE + lax.axis_index("core")
    bulk = EIGHTHS * 2 * CB
    row = lax.broadcasted_iota(jnp.int32, (EXTRA, LANES), 0)

    def fetch(block):
        block = jnp.clip(block, 0, 2 * PAIRS - 1)
        place = ((block >> 4) << 1) | ((block >> 1) & 1)
        column = (block >> 2) & (ZH - 1)
        start = pl.multiple_of(((place << 1) | (block & 1)) * CB, CB)
        data = table_ref[column, pl.ds(start, CB)]
        lines = table_ref[column, bulk:]
        lines = jnp.where(place == here, lines, jnp.zeros_like(lines))
        return data, lines

    for index in range(CHUNKS):
        place = index % EIGHTHS
        pair = ((place // CORE * ZH + zh) * CORE) + place % CORE
        tile = pair * X + index // EIGHTHS
        first = plan_ref[0, 0, tile]
        data, lines = fetch(first)
        data_second, lines_second = fetch(first + plan_ref[1, 0, tile])
        out_ref[index, :CB] = data
        out_ref[index, CB : 2 * CB] = data_second
        out_ref[index, 2 * CB :] = jnp.where(row < EXTRA // 2, lines, lines_second)


def chunk_place(chunk):
    return chunk


def scales(edge_ref, first_half, second_half, zl, length):
    row = lax.broadcasted_iota(jnp.int32, (EXTRA, LANES), 0)
    other = jnp.where(row < EXTRA // 2, first_half, second_half) > 0
    blocks = []
    for part in range(TMS):
        start = 2 * CB + part % X * EXTRA
        parts = edge_ref[part // X, start : start + EXTRA].astype(jnp.float32)
        whole = parts + (pltpu.roll(parts, EXTRA - 1, axis=0) + pltpu.roll(parts, EXTRA - 2, axis=0))
        blocks.append(jnp.where(other, pltpu.roll(whole, LANES - CB, axis=1), whole))
    average = sum(blocks[1:], blocks[0]) / TMS
    squares = pltpu.roll(average, LANES // 2, axis=1)
    apart = [block - average for block in blocks]
    spread = [piece * piece for piece in apart]
    power = squares / length + sum(spread[1:], spread[0]) / TMS
    scaling = lax.rsqrt(power + 1e-05)

    def wanted(places):
        piece = apart[places[0]]
        for zone in range(1, ZL):
            piece = jnp.where(zl == zone, apart[places[zone]], piece)
        return piece

    columns = [scaling, wanted([max(zone * X - 1, 0) for zone in range(ZL)])]
    columns += [wanted([zone * X + x for zone in range(ZL)]) for x in range(X)]
    columns.append(wanted([min(zone * X + X, TMS - 1) for zone in range(ZL)]))
    lane = lax.broadcasted_iota(jnp.int32, (EXTRA, LANES), 1)
    turned = []
    for base in (0, EXTRA // 2):
        packed = jnp.zeros((EXTRA, LANES), jnp.float32)
        for place, column in enumerate(columns):
            packed = jnp.where(row == place, column[base : base + 1], packed)
        turned.append(jnp.where(lane < CB, packed, 0.0))
    filler = jnp.zeros((LANES - 2 * EXTRA, LANES), jnp.float32)
    turned = jnp.transpose(jnp.concatenate(turned + [filler], axis=0))
    return turned[:CB, :EXTRA], turned[:CB, EXTRA : 2 * EXTRA]


def lag_kernel(length, plan_ref, data_ref, edge_ref, out_ref, wide_a, wide_b):
    zl = lax.axis_index("zl")
    pair = (lax.axis_index("y") * ZH + lax.axis_index("zh")) * CORE + lax.axis_index("core")
    tile = pair * X + lax.axis_index("x")
    alive = plan_ref[2, 0, tile]
    first_half = plan_ref[0, 0, tile] & 1
    second_half = (plan_ref[0, 0, tile] + plan_ref[1, 0, tile]) & 1
    width = (CHUNKS + 1) * LANES
    factor = 1.0 / math.sqrt(length * TMS)

    @pl.when(alive <= 0)
    def _():
        out_ref[...] = jnp.zeros_like(out_ref)

    @pl.when(alive > 0)
    def _():
        lane = lax.broadcasted_iota(jnp.int32, (CB, LANES), 1)
        zero = jnp.zeros((CB, LANES), jnp.bfloat16)
        first_scale, second_scale = scales(edge_ref, first_half, second_half, zl, length)

        def white(piece, scale, column):
            shifted = piece.astype(jnp.float32) + scale[:, column + 2 : column + 3]
            return (shifted * scale[:, 0:1]).astype(jnp.bfloat16)

        def first_chunk(chunk):
            return white(data_ref[chunk_place(chunk), :CB], first_scale, chunk // EIGHTHS)

        def second_chunk(chunk):
            if chunk < 0:
                piece = white(edge_ref[jnp.maximum(zl - 1, 0), CB : 2 * CB], second_scale, -1)
                return jnp.where(zl > 0, piece, zero)
            if chunk >= CHUNKS:
                piece = white(edge_ref[jnp.minimum(zl + 1, ZL - 1), :CB], second_scale, X)
                return jnp.where(zl < ZL - 1, piece, zero)
            return white(data_ref[chunk_place(chunk), CB : 2 * CB], second_scale, chunk // EIGHTHS)

        here = zero
        for chunk in range(CHUNKS + 1):
            past = here
            here = first_chunk(chunk) if chunk < CHUNKS else zero
            for step in range(MEDIUM):
                shift = step * FINE
                mixed = jnp.where(lane < LANES - shift, here, past)
                turned = pltpu.roll(mixed, shift, axis=1) if shift else here
                wide_a[step * CB : (step + 1) * CB, chunk * LANES : (chunk + 1) * LANES] = turned
        later = second_chunk(-1)
        for chunk in range(-1, CHUNKS + 1):
            here = later
            later = second_chunk(chunk + 1) if chunk < CHUNKS else zero
            for step in range(FINE):
                mixed = jnp.where(lane >= step, here, later)
                turned = pltpu.roll(mixed, LANES - step, axis=1) if step else here
                wide_b[
                    step * CB : (step + 1) * CB, (chunk + 1) * LANES : (chunk + 2) * LANES
                ] = turned
        for half in range(2):
            result = lax.dot_general(
                wide_a[...],
                wide_b[:, half * LANES : half * LANES + width],
                (((1,), (1,)), ((), ())),
                preferred_element_type=jnp.float32,
            )
            rounded = (result * factor).astype(jnp.bfloat16)
            for part in range(TMS // 2):
                out_ref[half * (TMS // 2) + part] = rounded[part * 2 * CB : (part + 1) * 2 * CB]


def finish_kernel(got_ref, out_hbm, out_ref, grid_ref, turn_ref, sems):
    lane = lax.broadcasted_iota(jnp.int32, (8, LANES), 1)
    copies = []
    for slot in range(X):
        total = got_ref[slot].astype(jnp.float32)
        for zl in range(1, ZL):
            total = total + got_ref[zl * X + slot].astype(jnp.float32)
        for g in range(2):
            grid_ref[g * 2 * CB : (g + 1) * 2 * CB] = total[:, g * LANES : (g + 1) * LANES]
        for half in range(2):
            parts = [
                [
                    grid_ref[pl.ds((2 * g + half) * CB + r, 8, stride=4), :]
                    for g in range(2)
                ]
                for r in range(4)
            ]
            for q in range(FINE):
                line = None
                for r in range(4):
                    piece = parts[r][q // 4]
                    shift = (CB * (r - q % 4)) % LANES
                    piece = pltpu.roll(piece, shift, axis=1) if shift else piece
                    line = piece if line is None else jnp.where(lane >= r * CB, piece, line)
                turn_ref[q * 8 : (q + 1) * 8, :] = line
            for k in range(8):
                out_ref[slot, half * 8 : half * 8 + 8, k * LANES : (k + 1) * LANES] = turn_ref[
                    pl.ds(k, 8, stride=8), :
                ]
        copies.append(pltpu.make_async_copy(out_ref.at[slot], out_hbm.at[slot], sems.at[slot]))
        copies[-1].start()
    for copy in copies:
        copy.wait()


def body(samples, tile_rows, tile_offsets, tile_live):
    length = samples.shape[1]
    bf16 = jnp.bfloat16
    parts, lines, plan = pl.pallas_call(
        split_kernel,
        out_shape=(
            jax.ShapeDtypeStruct((EIGHTHS, 2 * CB, LANES), bf16),
            jax.ShapeDtypeStruct((EXTRA, LANES), bf16),
            pltpu.SMEM((3, 1, LANES), jnp.int32),
        ),
        in_specs=[HBM] * 4,
        out_specs=(VMEM, VMEM, SMEM),
        scratch_shapes=[
            pltpu.VMEM(samples.shape, jnp.float32),
            pltpu.SemaphoreType.DMA((4,)),
        ],
        compiler_params=pltpu.CompilerParams(vmem_limit_bytes=3 * MIB),
        name="split",
    )(
        *(
            pltpu.with_memory_space_constraint(array, pltpu.HBM)
            for array in (samples, tile_rows[None], tile_offsets[None], tile_live[None])
        )
    )
    with jax.named_scope("spread_y"):
        table = lax.all_to_all(parts, ("y", "core"), 0, 0, tiled=True)
    with jax.named_scope("spread_z"):
        table = jnp.concatenate([table.reshape(EIGHTHS * 2 * CB, LANES), lines])
        table = lax.all_gather(table, "zh")
    chosen = pl.pallas_call(
        select_kernel,
        out_shape=jax.ShapeDtypeStruct((CHUNKS, ROWS, LANES), bf16),
        in_specs=[SMEM, VMEM],
        out_specs=VMEM,
        compiler_params=pltpu.CompilerParams(vmem_limit_bytes=6 * MIB),
        name="select",
    )(pltpu.with_memory_space_constraint(plan, pltpu.SMEM), table)
    with jax.named_scope("collect"):
        data = lax.all_to_all(chosen, ("x", "y", "core"), 0, 0, tiled=True)
    with jax.named_scope("edges"):
        sums = jnp.sum(data[:, 2 * CB :].reshape(X, EIGHTHS, EXTRA, LANES), axis=1)
        sums = sums.reshape(X * EXTRA, LANES)
        edges = jnp.concatenate(
            [data[chunk_place(0), CB : 2 * CB], data[chunk_place(CHUNKS - 1), CB : 2 * CB], sums]
        )
        edges = lax.all_to_all(
            jnp.broadcast_to(edges[None], (ZL,) + edges.shape), "zl", 0, 0, tiled=True
        )
    partial = pl.pallas_call(
        lambda *refs: lag_kernel(length, *refs),
        out_shape=jax.ShapeDtypeStruct((TMS, 2 * CB, FINE * CB), bf16),
        in_specs=[SMEM, VMEM, VMEM],
        out_specs=VMEM,
        scratch_shapes=[
            pltpu.VMEM((MEDIUM * CB, (CHUNKS + 1) * LANES), bf16),
            pltpu.VMEM((FINE * CB, (CHUNKS + 2) * LANES), bf16),
        ],
        compiler_params=pltpu.CompilerParams(vmem_limit_bytes=16 * MIB),
        name="lags",
    )(pltpu.with_memory_space_constraint(plan, pltpu.SMEM), data, edges)
    with jax.named_scope("reduce"):
        got = lax.all_to_all(partial, ("zl", "x"), 0, 0, tiled=True)
    return pl.pallas_call(
        finish_kernel,
        out_shape=jax.ShapeDtypeStruct((X, 2 * FINE, CB * CB), jnp.float32),
        in_specs=[VMEM],
        out_specs=HBM,
        scratch_shapes=[
            pltpu.VMEM((X, 2 * FINE, CB * CB), jnp.float32),
            pltpu.VMEM((4 * CB, LANES), jnp.float32),
            pltpu.VMEM((FINE * 8, LANES), jnp.float32),
            pltpu.SemaphoreType.DMA((X,)),
        ],
        compiler_params=pltpu.CompilerParams(vmem_limit_bytes=4 * MIB),
        name="finish",
    )(got)


def solution(mesh):
    devices = mesh.devices.reshape(Y, ZH, CORE, ZL, X)
    spread = Mesh(devices, AXES)
    pair, tm = ("y", "zh", "core"), ("zl", "x")
    return jax.shard_map(
        body,
        mesh=spread,
        in_specs=(P(pair, tm), P(), P(), P()),
        out_specs=P(pair, tm, None),
        check_vma=False,
    )
```

```python
import math

import jax
import jax.numpy as jnp
from jax import lax
from jax.experimental import pallas as pl
from jax.experimental.pallas import tpu as pltpu
from jax.sharding import Mesh
from jax.sharding import PartitionSpec as P

CB = 32
LAG = 128
LANES = 128
Y, ZH, CORE, ZL, X = 4, 4, 2, 4, 4
AXES = ("y", "zh", "core", "zl", "x")
PAIRS = Y * ZH * CORE
TMS = ZL * X
EIGHTHS = Y * CORE
CHUNKS = X * EIGHTHS
FINE = 8
MEDIUM = LANES // FINE
EXTRA = 8
STRIPS = 4
ROWS = 2 * CB + EXTRA
MIB = 1 << 20

VMEM = pl.BlockSpec(memory_space=pltpu.VMEM)
SMEM = pl.BlockSpec(memory_space=pltpu.SMEM)
HBM = pl.BlockSpec(memory_space=pltpu.HBM)


def split_kernel(x_hbm, rows_hbm, offsets_hbm, live_hbm, out_ref, extra_ref, plan_ref, x_ref, sems):
    rows, length = x_ref.shape
    copies = []
    for strip in range(STRIPS):
        part = pl.ds(strip * (rows // STRIPS), rows // STRIPS)
        copies.append(pltpu.make_async_copy(x_hbm.at[part], x_ref.at[part], sems.at[strip]))
    for place, ref in enumerate((rows_hbm, offsets_hbm, live_hbm)):
        copies.append(pltpu.make_async_copy(ref, plan_ref.at[place], sems.at[STRIPS + place]))
    for copy in copies:
        copy.start()
    for copy in copies[:STRIPS]:
        copy.wait()
    mean = jnp.sum(x_ref[...], axis=1, keepdims=True) / length
    spread = jnp.zeros((rows, 1), jnp.float32)
    for part in range(EIGHTHS):
        piece = x_ref[:, part * LANES : (part + 1) * LANES] - mean
        spread = spread + jnp.sum(piece * piece, axis=1, keepdims=True)
        out_ref[part] = piece.astype(jnp.bfloat16)
    lane = lax.broadcasted_iota(jnp.int32, (rows, LANES), 1)
    channel = lax.broadcasted_iota(jnp.int32, (rows, LANES), 0)
    placed = jnp.where(lane == channel, mean, jnp.where(lane == channel + rows, spread, 0.0))
    line = jnp.sum(placed, axis=0, keepdims=True)
    high = line.astype(jnp.bfloat16).astype(jnp.float32)
    middle = (line - high).astype(jnp.bfloat16).astype(jnp.float32)
    low = line - high - middle
    row = lax.broadcasted_iota(jnp.int32, (EXTRA, LANES), 0) % (EXTRA // 2)
    lines = jnp.where(row == 0, high, jnp.where(row == 1, middle, jnp.where(row == 2, low, 0.0)))
    extra_ref[...] = lines.astype(jnp.bfloat16)
    for copy in copies[STRIPS:]:
        copy.wait()


def select_kernel(plan_ref, table_ref, out_ref):
    zh = lax.axis_index("zh")
    here = lax.axis_index("y") * CORE + lax.axis_index("core")
    bulk = EIGHTHS * 2 * CB
    row = lax.broadcasted_iota(jnp.int32, (EXTRA, LANES), 0)

    def fetch(block):
        block = jnp.clip(block, 0, 2 * PAIRS - 1)
        place = ((block >> 4) << 1) | ((block >> 1) & 1)
        column = (block >> 2) & (ZH - 1)
        start = pl.multiple_of(((place << 1) | (block & 1)) * CB, CB)
        data = table_ref[column, pl.ds(start, CB)]
        lines = table_ref[column, bulk:]
        lines = jnp.where(place == here, lines, jnp.zeros_like(lines))
        return data, lines

    for index in range(CHUNKS):
        place = index // X
        pair = ((place // CORE * ZH + zh) * CORE) + place % CORE
        tile = pair * X + index % X
        first = plan_ref[0, 0, tile]
        data, lines = fetch(first)
        data_second, lines_second = fetch(first + plan_ref[1, 0, tile])
        out_ref[index, :CB] = data
        out_ref[index, CB : 2 * CB] = data_second
        out_ref[index, 2 * CB :] = jnp.where(row < EXTRA // 2, lines, lines_second)


def chunk_place(chunk):
    return chunk % EIGHTHS * X + chunk // EIGHTHS


def scales(edge_ref, first_half, second_half, zl, length):
    row = lax.broadcasted_iota(jnp.int32, (EXTRA, LANES), 0)
    other = jnp.where(row < EXTRA // 2, first_half, second_half) > 0
    blocks = []
    for part in range(TMS):
        start = 2 * CB + part % X * EXTRA
        parts = edge_ref[part // X, start : start + EXTRA].astype(jnp.float32)
        whole = parts + (pltpu.roll(parts, EXTRA - 1, axis=0) + pltpu.roll(parts, EXTRA - 2, axis=0))
        blocks.append(jnp.where(other, pltpu.roll(whole, LANES - CB, axis=1), whole))
    average = sum(blocks[1:], blocks[0]) / TMS
    squares = pltpu.roll(average, LANES // 2, axis=1)
    apart = [block - average for block in blocks]
    spread = [piece * piece for piece in apart]
    power = squares / length + sum(spread[1:], spread[0]) / TMS
    scaling = lax.rsqrt(power + 1e-05)

    def wanted(places):
        piece = apart[places[0]]
        for zone in range(1, ZL):
            piece = jnp.where(zl == zone, apart[places[zone]], piece)
        return piece

    columns = [scaling, wanted([max(zone * X - 1, 0) for zone in range(ZL)])]
    columns += [wanted([zone * X + x for zone in range(ZL)]) for x in range(X)]
    columns.append(wanted([min(zone * X + X, TMS - 1) for zone in range(ZL)]))
    lane = lax.broadcasted_iota(jnp.int32, (EXTRA, LANES), 1)
    turned = []
    for base in (0, EXTRA // 2):
        packed = jnp.zeros((EXTRA, LANES), jnp.float32)
        for place, column in enumerate(columns):
            packed = jnp.where(row == place, column[base : base + 1], packed)
        turned.append(jnp.where(lane < CB, packed, 0.0))
    filler = jnp.zeros((LANES - 2 * EXTRA, LANES), jnp.float32)
    turned = jnp.transpose(jnp.concatenate(turned + [filler], axis=0))
    return turned[:CB, :EXTRA], turned[:CB, EXTRA : 2 * EXTRA]


def lag_kernel(length, plan_ref, data_ref, edge_ref, out_ref, wide_a, wide_b):
    zl = lax.axis_index("zl")
    pair = (lax.axis_index("y") * ZH + lax.axis_index("zh")) * CORE + lax.axis_index("core")
    tile = pair * X + lax.axis_index("x")
    alive = plan_ref[2, 0, tile]
    first_half = plan_ref[0, 0, tile] & 1
    second_half = (plan_ref[0, 0, tile] + plan_ref[1, 0, tile]) & 1
    width = (CHUNKS + 1) * LANES
    factor = 1.0 / math.sqrt(length * TMS)

    @pl.when(alive <= 0)
    def _():
        out_ref[...] = jnp.zeros_like(out_ref)

    @pl.when(alive > 0)
    def _():
        lane = lax.broadcasted_iota(jnp.int32, (CB, LANES), 1)
        zero = jnp.zeros((CB, LANES), jnp.bfloat16)
        first_scale, second_scale = scales(edge_ref, first_half, second_half, zl, length)

        first_by = first_scale[:, 0:1] * factor
        second_by = second_scale[:, 0:1]

        def white(piece, scale, column, by):
            shifted = piece.astype(jnp.float32) + scale[:, column + 2 : column + 3]
            return (shifted * by).astype(jnp.bfloat16)

        def first_chunk(chunk):
            return white(data_ref[chunk_place(chunk), :CB], first_scale, chunk // EIGHTHS, first_by)

        def second_chunk(chunk):
            if chunk < 0:
                piece = white(edge_ref[jnp.maximum(zl - 1, 0), CB : 2 * CB], second_scale, -1, second_by)
                return jnp.where(zl > 0, piece, zero)
            if chunk >= CHUNKS:
                piece = white(edge_ref[jnp.minimum(zl + 1, ZL - 1), :CB], second_scale, X, second_by)
                return jnp.where(zl < ZL - 1, piece, zero)
            return white(data_ref[chunk_place(chunk), CB : 2 * CB], second_scale, chunk // EIGHTHS, second_by)

        here = zero
        for chunk in range(CHUNKS + 1):
            past = here
            here = first_chunk(chunk) if chunk < CHUNKS else zero
            for step in range(MEDIUM):
                shift = step * FINE
                mixed = jnp.where(lane < LANES - shift, here, past)
                turned = pltpu.roll(mixed, shift, axis=1) if shift else here
                wide_a[step * CB : (step + 1) * CB, chunk * LANES : (chunk + 1) * LANES] = turned
        later = second_chunk(-1)
        for chunk in range(-1, CHUNKS + 1):
            here = later
            later = second_chunk(chunk + 1) if chunk < CHUNKS else zero
            for step in range(FINE):
                mixed = jnp.where(lane >= step, here, later)
                turned = pltpu.roll(mixed, LANES - step, axis=1) if step else here
                wide_b[
                    step * CB : (step + 1) * CB, (chunk + 1) * LANES : (chunk + 2) * LANES
                ] = turned
        for half in range(2):
            result = lax.dot_general(
                wide_a[...],
                wide_b[:, half * LANES : half * LANES + width],
                (((1,), (1,)), ((), ())),
                preferred_element_type=jnp.float32,
            )
            rounded = result.astype(jnp.bfloat16)
            for part in range(TMS // 2):
                out_ref[half * (TMS // 2) + part] = rounded[part * 2 * CB : (part + 1) * 2 * CB]


def finish_kernel(got_ref, out_hbm, out_ref, grid_ref, turn_ref, sems):
    lane = lax.broadcasted_iota(jnp.int32, (8, LANES), 1)
    copies = []
    for slot in range(X):
        total = got_ref[slot].astype(jnp.float32)
        for zl in range(1, ZL):
            total = total + got_ref[zl * X + slot].astype(jnp.float32)
        for g in range(2):
            grid_ref[g * 2 * CB : (g + 1) * 2 * CB] = total[:, g * LANES : (g + 1) * LANES]
        for half in range(2):
            parts = [
                [
                    grid_ref[pl.ds((2 * g + half) * CB + r, 8, stride=4), :]
                    for g in range(2)
                ]
                for r in range(4)
            ]
            for q in range(FINE):
                line = None
                for r in range(4):
                    piece = parts[r][q // 4]
                    shift = (CB * (r - q % 4)) % LANES
                    piece = pltpu.roll(piece, shift, axis=1) if shift else piece
                    line = piece if line is None else jnp.where(lane >= r * CB, piece, line)
                turn_ref[q * 8 : (q + 1) * 8, :] = line
            for k in range(8):
                out_ref[slot, half * 8 : half * 8 + 8, k * LANES : (k + 1) * LANES] = turn_ref[
                    pl.ds(k, 8, stride=8), :
                ]
        copies.append(pltpu.make_async_copy(out_ref.at[slot], out_hbm.at[slot], sems.at[slot]))
        copies[-1].start()
    for copy in copies:
        copy.wait()


def body(samples, tile_rows, tile_offsets, tile_live):
    length = samples.shape[1]
    bf16 = jnp.bfloat16
    parts, lines, plan = pl.pallas_call(
        split_kernel,
        out_shape=(
            jax.ShapeDtypeStruct((EIGHTHS, 2 * CB, LANES), bf16),
            jax.ShapeDtypeStruct((EXTRA, LANES), bf16),
            pltpu.SMEM((3, 1, LANES), jnp.int32),
        ),
        in_specs=[HBM] * 4,
        out_specs=(VMEM, VMEM, SMEM),
        scratch_shapes=[
            pltpu.VMEM(samples.shape, jnp.float32),
            pltpu.SemaphoreType.DMA((STRIPS + 3,)),
        ],
        compiler_params=pltpu.CompilerParams(vmem_limit_bytes=3 * MIB),
        name="split",
    )(
        *(
            pltpu.with_memory_space_constraint(array, pltpu.HBM)
            for array in (samples, tile_rows[None], tile_offsets[None], tile_live[None])
        )
    )
    with jax.named_scope("spread_y"):
        table = lax.all_to_all(parts, ("y", "core"), 0, 0, tiled=True)
    with jax.named_scope("spread_z"):
        table = jnp.concatenate([table.reshape(EIGHTHS * 2 * CB, LANES), lines])
        table = lax.all_gather(table, "zh")
    chosen = pl.pallas_call(
        select_kernel,
        out_shape=jax.ShapeDtypeStruct((CHUNKS, ROWS, LANES), bf16),
        in_specs=[SMEM, VMEM],
        out_specs=VMEM,
        compiler_params=pltpu.CompilerParams(vmem_limit_bytes=6 * MIB),
        name="select",
    )(pltpu.with_memory_space_constraint(plan, pltpu.SMEM), table)
    with jax.named_scope("collect"):
        data = lax.all_to_all(chosen, ("y", "core", "x"), 0, 0, tiled=True)
    with jax.named_scope("edges"):
        sums = jnp.sum(data[:, 2 * CB :].reshape(EIGHTHS, X * EXTRA, LANES), axis=0)
        edges = jnp.concatenate(
            [data[chunk_place(0), CB : 2 * CB], data[chunk_place(CHUNKS - 1), CB : 2 * CB], sums]
        )
        edges = lax.all_to_all(
            jnp.broadcast_to(edges[None], (ZL,) + edges.shape), "zl", 0, 0, tiled=True
        )
    partial = pl.pallas_call(
        lambda *refs: lag_kernel(length, *refs),
        out_shape=jax.ShapeDtypeStruct((TMS, 2 * CB, FINE * CB), bf16),
        in_specs=[SMEM, VMEM, VMEM],
        out_specs=VMEM,
        scratch_shapes=[
            pltpu.VMEM((MEDIUM * CB, (CHUNKS + 1) * LANES), bf16),
            pltpu.VMEM((FINE * CB, (CHUNKS + 2) * LANES), bf16),
        ],
        compiler_params=pltpu.CompilerParams(vmem_limit_bytes=16 * MIB),
        name="lags",
    )(pltpu.with_memory_space_constraint(plan, pltpu.SMEM), data, edges)
    with jax.named_scope("reduce"):
        got = lax.all_to_all(partial, ("zl", "x"), 0, 0, tiled=True)
    return pl.pallas_call(
        finish_kernel,
        out_shape=jax.ShapeDtypeStruct((X, 2 * FINE, CB * CB), jnp.float32),
        in_specs=[VMEM],
        out_specs=HBM,
        scratch_shapes=[
            pltpu.VMEM((X, 2 * FINE, CB * CB), jnp.float32),
            pltpu.VMEM((4 * CB, LANES), jnp.float32),
            pltpu.VMEM((FINE * 8, LANES), jnp.float32),
            pltpu.SemaphoreType.DMA((X,)),
        ],
        compiler_params=pltpu.CompilerParams(vmem_limit_bytes=4 * MIB),
        name="finish",
    )(got)


def solution(mesh):
    devices = mesh.devices.reshape(Y, ZH, CORE, ZL, X)
    spread = Mesh(devices, AXES)
    pair, tm = ("y", "zh", "core"), ("zl", "x")
    return jax.shard_map(
        body,
        mesh=spread,
        in_specs=(P(pair, tm), P(), P(), P()),
        out_specs=P(pair, tm, None),
        check_vma=False,
    )
```

```python
import math

import jax
import jax.numpy as jnp
from jax import lax
from jax.experimental import pallas as pl
from jax.experimental.pallas import tpu as pltpu
from jax.sharding import Mesh
from jax.sharding import PartitionSpec as P

CB = 32
LAG = 128
LANES = 128
Y, ZH, CORE, ZL, X = 4, 4, 2, 4, 4
AXES = ("y", "zh", "core", "zl", "x")
PAIRS = Y * ZH * CORE
TMS = ZL * X
EIGHTHS = Y * CORE
CHUNKS = X * EIGHTHS
FINE = 8
MEDIUM = LANES // FINE
EXTRA = 8
STRIPS = 4
ROWS = 2 * CB + EXTRA
MIB = 1 << 20

VMEM = pl.BlockSpec(memory_space=pltpu.VMEM)
SMEM = pl.BlockSpec(memory_space=pltpu.SMEM)
HBM = pl.BlockSpec(memory_space=pltpu.HBM)


def split_kernel(x_hbm, rows_hbm, offsets_hbm, live_hbm, out_ref, extra_ref, plan_ref, x_ref, sems):
    rows, length = x_ref.shape
    copies = []
    for strip in range(STRIPS):
        part = pl.ds(strip * (rows // STRIPS), rows // STRIPS)
        copies.append(pltpu.make_async_copy(x_hbm.at[part], x_ref.at[part], sems.at[strip]))
    for place, ref in enumerate((rows_hbm, offsets_hbm, live_hbm)):
        copies.append(pltpu.make_async_copy(ref, plan_ref.at[place], sems.at[STRIPS + place]))
    for copy in copies:
        copy.start()
    for copy in copies[:STRIPS]:
        copy.wait()
    mean = jnp.sum(x_ref[...], axis=1, keepdims=True) / length
    spread = jnp.zeros((rows, 1), jnp.float32)
    for part in range(EIGHTHS):
        piece = x_ref[:, part * LANES : (part + 1) * LANES] - mean
        spread = spread + jnp.sum(piece * piece, axis=1, keepdims=True)
        out_ref[part] = piece.astype(jnp.bfloat16)
    lane = lax.broadcasted_iota(jnp.int32, (rows, LANES), 1)
    channel = lax.broadcasted_iota(jnp.int32, (rows, LANES), 0)
    placed = jnp.where(lane == channel, mean, jnp.where(lane == channel + rows, spread, 0.0))
    line = jnp.sum(placed, axis=0, keepdims=True)
    high = line.astype(jnp.bfloat16).astype(jnp.float32)
    middle = (line - high).astype(jnp.bfloat16).astype(jnp.float32)
    low = line - high - middle
    row = lax.broadcasted_iota(jnp.int32, (EXTRA, LANES), 0) % (EXTRA // 2)
    lines = jnp.where(row == 0, high, jnp.where(row == 1, middle, jnp.where(row == 2, low, 0.0)))
    extra_ref[...] = lines.astype(jnp.bfloat16)
    for copy in copies[STRIPS:]:
        copy.wait()


def select_kernel(plan_ref, table_ref, out_ref):
    zh = lax.axis_index("zh")
    here = lax.axis_index("core") * Y + lax.axis_index("y")
    bulk = EIGHTHS * 2 * CB
    row = lax.broadcasted_iota(jnp.int32, (EXTRA, LANES), 0)

    def fetch(block):
        block = jnp.clip(block, 0, 2 * PAIRS - 1)
        place = (((block >> 1) & 1) << 2) | (block >> 4)
        column = (block >> 2) & (ZH - 1)
        start = pl.multiple_of(((place << 1) | (block & 1)) * CB, CB)
        data = table_ref[column, pl.ds(start, CB)]
        lines = table_ref[column, bulk:]
        lines = jnp.where(place == here, lines, jnp.zeros_like(lines))
        return data, lines

    for index in range(CHUNKS):
        place = index // X
        pair = ((place % Y * ZH + zh) * CORE) + place // Y
        tile = pair * X + index % X
        first = plan_ref[0, 0, tile]
        data, lines = fetch(first)
        data_second, lines_second = fetch(first + plan_ref[1, 0, tile])
        out_ref[index, :CB] = data
        out_ref[index, CB : 2 * CB] = data_second
        out_ref[index, 2 * CB :] = jnp.where(row < EXTRA // 2, lines, lines_second)


def chunk_place(chunk):
    return chunk % EIGHTHS * X + chunk // EIGHTHS


def scales(edge_ref, first_half, second_half, zl, length):
    row = lax.broadcasted_iota(jnp.int32, (EXTRA, LANES), 0)
    other = jnp.where(row < EXTRA // 2, first_half, second_half) > 0
    blocks = []
    for part in range(TMS):
        start = 2 * CB + part % X * EXTRA
        parts = edge_ref[part // X, start : start + EXTRA].astype(jnp.float32)
        whole = parts + (pltpu.roll(parts, EXTRA - 1, axis=0) + pltpu.roll(parts, EXTRA - 2, axis=0))
        blocks.append(jnp.where(other, pltpu.roll(whole, LANES - CB, axis=1), whole))
    average = sum(blocks[1:], blocks[0]) / TMS
    squares = pltpu.roll(average, LANES // 2, axis=1)
    apart = [block - average for block in blocks]
    spread = [piece * piece for piece in apart]
    power = squares / length + sum(spread[1:], spread[0]) / TMS
    scaling = lax.rsqrt(power + 1e-05)

    def wanted(places):
        piece = apart[places[0]]
        for zone in range(1, ZL):
            piece = jnp.where(zl == zone, apart[places[zone]], piece)
        return piece

    columns = [scaling, wanted([max(zone * X - 1, 0) for zone in range(ZL)])]
    columns += [wanted([zone * X + x for zone in range(ZL)]) for x in range(X)]
    columns.append(wanted([min(zone * X + X, TMS - 1) for zone in range(ZL)]))
    lane = lax.broadcasted_iota(jnp.int32, (EXTRA, LANES), 1)
    turned = []
    for base in (0, EXTRA // 2):
        packed = jnp.zeros((EXTRA, LANES), jnp.float32)
        for place, column in enumerate(columns):
            packed = jnp.where(row == place, column[base : base + 1], packed)
        turned.append(jnp.where(lane < CB, packed, 0.0))
    filler = jnp.zeros((LANES - 2 * EXTRA, LANES), jnp.float32)
    turned = jnp.transpose(jnp.concatenate(turned + [filler], axis=0))
    return turned[:CB, :EXTRA], turned[:CB, EXTRA : 2 * EXTRA]


def lag_kernel(length, plan_ref, data_ref, edge_ref, out_ref, wide_a, wide_b):
    zl = lax.axis_index("zl")
    pair = (lax.axis_index("y") * ZH + lax.axis_index("zh")) * CORE + lax.axis_index("core")
    tile = pair * X + lax.axis_index("x")
    alive = plan_ref[2, 0, tile]
    first_half = plan_ref[0, 0, tile] & 1
    second_half = (plan_ref[0, 0, tile] + plan_ref[1, 0, tile]) & 1
    width = (CHUNKS + 1) * LANES
    factor = 1.0 / math.sqrt(length * TMS)

    @pl.when(alive <= 0)
    def _():
        out_ref[...] = jnp.zeros_like(out_ref)

    @pl.when(alive > 0)
    def _():
        lane = lax.broadcasted_iota(jnp.int32, (CB, LANES), 1)
        zero = jnp.zeros((CB, LANES), jnp.bfloat16)
        first_scale, second_scale = scales(edge_ref, first_half, second_half, zl, length)

        first_by = first_scale[:, 0:1] * factor
        second_by = second_scale[:, 0:1]

        def white(piece, scale, column, by):
            shifted = piece.astype(jnp.float32) + scale[:, column + 2 : column + 3]
            return (shifted * by).astype(jnp.bfloat16)

        def first_chunk(chunk):
            return white(data_ref[chunk_place(chunk), :CB], first_scale, chunk // EIGHTHS, first_by)

        def second_chunk(chunk):
            if chunk < 0:
                piece = white(edge_ref[jnp.maximum(zl - 1, 0), CB : 2 * CB], second_scale, -1, second_by)
                return jnp.where(zl > 0, piece, zero)
            if chunk >= CHUNKS:
                piece = white(edge_ref[jnp.minimum(zl + 1, ZL - 1), :CB], second_scale, X, second_by)
                return jnp.where(zl < ZL - 1, piece, zero)
            return white(data_ref[chunk_place(chunk), CB : 2 * CB], second_scale, chunk // EIGHTHS, second_by)

        here = zero
        for chunk in range(CHUNKS + 1):
            past = here
            here = first_chunk(chunk) if chunk < CHUNKS else zero
            for step in range(MEDIUM):
                shift = step * FINE
                mixed = jnp.where(lane < LANES - shift, here, past)
                turned = pltpu.roll(mixed, shift, axis=1) if shift else here
                wide_a[step * CB : (step + 1) * CB, chunk * LANES : (chunk + 1) * LANES] = turned
        later = second_chunk(-1)
        for chunk in range(-1, CHUNKS + 1):
            here = later
            later = second_chunk(chunk + 1) if chunk < CHUNKS else zero
            for step in range(FINE):
                mixed = jnp.where(lane >= step, here, later)
                turned = pltpu.roll(mixed, LANES - step, axis=1) if step else here
                wide_b[
                    step * CB : (step + 1) * CB, (chunk + 1) * LANES : (chunk + 2) * LANES
                ] = turned
        for half in range(2):
            result = lax.dot_general(
                wide_a[...],
                wide_b[:, half * LANES : half * LANES + width],
                (((1,), (1,)), ((), ())),
                preferred_element_type=jnp.float32,
            )
            rounded = result.astype(jnp.bfloat16)
            for part in range(TMS // 2):
                out_ref[half * (TMS // 2) + part] = rounded[part * 2 * CB : (part + 1) * 2 * CB]


def finish_kernel(got_ref, out_hbm, out_ref, grid_ref, turn_ref, sems):
    lane = lax.broadcasted_iota(jnp.int32, (8, LANES), 1)
    copies = []
    for slot in range(X):
        total = got_ref[slot].astype(jnp.float32)
        for zl in range(1, ZL):
            total = total + got_ref[zl * X + slot].astype(jnp.float32)
        for g in range(2):
            grid_ref[g * 2 * CB : (g + 1) * 2 * CB] = total[:, g * LANES : (g + 1) * LANES]
        for half in range(2):
            parts = [
                [
                    grid_ref[pl.ds((2 * g + half) * CB + r, 8, stride=4), :]
                    for g in range(2)
                ]
                for r in range(4)
            ]
            for q in range(FINE):
                line = None
                for r in range(4):
                    piece = parts[r][q // 4]
                    shift = (CB * (r - q % 4)) % LANES
                    piece = pltpu.roll(piece, shift, axis=1) if shift else piece
                    line = piece if line is None else jnp.where(lane >= r * CB, piece, line)
                turn_ref[q * 8 : (q + 1) * 8, :] = line
            for k in range(8):
                out_ref[slot, half * 8 : half * 8 + 8, k * LANES : (k + 1) * LANES] = turn_ref[
                    pl.ds(k, 8, stride=8), :
                ]
        copies.append(pltpu.make_async_copy(out_ref.at[slot], out_hbm.at[slot], sems.at[slot]))
        copies[-1].start()
    for copy in copies:
        copy.wait()


def body(samples, tile_rows, tile_offsets, tile_live):
    length = samples.shape[1]
    bf16 = jnp.bfloat16
    parts, lines, plan = pl.pallas_call(
        split_kernel,
        out_shape=(
            jax.ShapeDtypeStruct((EIGHTHS, 2 * CB, LANES), bf16),
            jax.ShapeDtypeStruct((EXTRA, LANES), bf16),
            pltpu.SMEM((3, 1, LANES), jnp.int32),
        ),
        in_specs=[HBM] * 4,
        out_specs=(VMEM, VMEM, SMEM),
        scratch_shapes=[
            pltpu.VMEM(samples.shape, jnp.float32),
            pltpu.SemaphoreType.DMA((STRIPS + 3,)),
        ],
        compiler_params=pltpu.CompilerParams(vmem_limit_bytes=3 * MIB),
        name="split",
    )(
        *(
            pltpu.with_memory_space_constraint(array, pltpu.HBM)
            for array in (samples, tile_rows[None], tile_offsets[None], tile_live[None])
        )
    )
    with jax.named_scope("spread_y"):
        table = lax.all_to_all(parts, ("core", "y"), 0, 0, tiled=True)
    with jax.named_scope("spread_z"):
        table = jnp.concatenate([table.reshape(EIGHTHS * 2 * CB, LANES), lines])
        table = lax.all_gather(table, "zh")
    chosen = pl.pallas_call(
        select_kernel,
        out_shape=jax.ShapeDtypeStruct((CHUNKS, ROWS, LANES), bf16),
        in_specs=[SMEM, VMEM],
        out_specs=VMEM,
        compiler_params=pltpu.CompilerParams(vmem_limit_bytes=6 * MIB),
        name="select",
    )(pltpu.with_memory_space_constraint(plan, pltpu.SMEM), table)
    with jax.named_scope("collect"):
        data = lax.all_to_all(chosen, ("core", "y", "x"), 0, 0, tiled=True)
    with jax.named_scope("edges"):
        sums = jnp.sum(data[:, 2 * CB :].reshape(EIGHTHS, X * EXTRA, LANES), axis=0)
        edges = jnp.concatenate(
            [data[chunk_place(0), CB : 2 * CB], data[chunk_place(CHUNKS - 1), CB : 2 * CB], sums]
        )
        edges = lax.all_to_all(
            jnp.broadcast_to(edges[None], (ZL,) + edges.shape), "zl", 0, 0, tiled=True
        )
    partial = pl.pallas_call(
        lambda *refs: lag_kernel(length, *refs),
        out_shape=jax.ShapeDtypeStruct((TMS, 2 * CB, FINE * CB), bf16),
        in_specs=[SMEM, VMEM, VMEM],
        out_specs=VMEM,
        scratch_shapes=[
            pltpu.VMEM((MEDIUM * CB, (CHUNKS + 1) * LANES), bf16),
            pltpu.VMEM((FINE * CB, (CHUNKS + 2) * LANES), bf16),
        ],
        compiler_params=pltpu.CompilerParams(vmem_limit_bytes=16 * MIB),
        name="lags",
    )(pltpu.with_memory_space_constraint(plan, pltpu.SMEM), data, edges)
    with jax.named_scope("reduce"):
        got = lax.all_to_all(partial, ("zl", "x"), 0, 0, tiled=True)
    return pl.pallas_call(
        finish_kernel,
        out_shape=jax.ShapeDtypeStruct((X, 2 * FINE, CB * CB), jnp.float32),
        in_specs=[VMEM],
        out_specs=HBM,
        scratch_shapes=[
            pltpu.VMEM((X, 2 * FINE, CB * CB), jnp.float32),
            pltpu.VMEM((4 * CB, LANES), jnp.float32),
            pltpu.VMEM((FINE * 8, LANES), jnp.float32),
            pltpu.SemaphoreType.DMA((X,)),
        ],
        compiler_params=pltpu.CompilerParams(vmem_limit_bytes=4 * MIB),
        name="finish",
    )(got)


def solution(mesh):
    devices = mesh.devices.reshape(Y, ZH, CORE, ZL, X)
    spread = Mesh(devices, AXES)
    pair, tm = ("y", "zh", "core"), ("zl", "x")
    return jax.shard_map(
        body,
        mesh=spread,
        in_specs=(P(pair, tm), P(), P(), P()),
        out_specs=P(pair, tm, None),
        check_vma=False,
    )
```

```python
import math

import jax
import jax.numpy as jnp
from jax import lax
from jax.experimental import pallas as pl
from jax.experimental.pallas import tpu as pltpu
from jax.sharding import Mesh
from jax.sharding import PartitionSpec as P

CB = 32
LAG = 128
LANES = 128
Y, ZH, CORE, ZL, X = 4, 4, 2, 4, 4
AXES = ("y", "zh", "core", "zl", "x")
PAIRS = Y * ZH * CORE
TMS = ZL * X
EIGHTHS = Y * CORE
CHUNKS = X * EIGHTHS
FINE = 8
MEDIUM = LANES // FINE
EXTRA = 8
STRIPS = 4
ROWS = 2 * CB + EXTRA
MIB = 1 << 20

VMEM = pl.BlockSpec(memory_space=pltpu.VMEM)
SMEM = pl.BlockSpec(memory_space=pltpu.SMEM)
HBM = pl.BlockSpec(memory_space=pltpu.HBM)


def split_kernel(x_hbm, rows_hbm, offsets_hbm, live_hbm, out_ref, extra_ref, plan_ref, x_ref, sems):
    rows, length = x_ref.shape
    copies = []
    for strip in range(STRIPS):
        part = pl.ds(strip * (rows // STRIPS), rows // STRIPS)
        copies.append(pltpu.make_async_copy(x_hbm.at[part], x_ref.at[part], sems.at[strip]))
    for place, ref in enumerate((rows_hbm, offsets_hbm, live_hbm)):
        copies.append(pltpu.make_async_copy(ref, plan_ref.at[place], sems.at[STRIPS + place]))
    for copy in copies:
        copy.start()
    for copy in copies[:STRIPS]:
        copy.wait()
    mean = jnp.sum(x_ref[...], axis=1, keepdims=True) / length
    spread = jnp.zeros((rows, 1), jnp.float32)
    for part in range(EIGHTHS):
        piece = x_ref[:, part * LANES : (part + 1) * LANES] - mean
        spread = spread + jnp.sum(piece * piece, axis=1, keepdims=True)
        out_ref[part] = piece.astype(jnp.bfloat16)
    lane = lax.broadcasted_iota(jnp.int32, (rows, LANES), 1)
    channel = lax.broadcasted_iota(jnp.int32, (rows, LANES), 0)
    placed = jnp.where(lane == channel, mean, jnp.where(lane == channel + rows, spread, 0.0))
    line = jnp.sum(placed, axis=0, keepdims=True)
    high = line.astype(jnp.bfloat16).astype(jnp.float32)
    middle = (line - high).astype(jnp.bfloat16).astype(jnp.float32)
    low = line - high - middle
    row = lax.broadcasted_iota(jnp.int32, (EXTRA, LANES), 0) % (EXTRA // 2)
    lines = jnp.where(row == 0, high, jnp.where(row == 1, middle, jnp.where(row == 2, low, 0.0)))
    extra_ref[...] = lines.astype(jnp.bfloat16)
    for copy in copies[STRIPS:]:
        copy.wait()


def select_kernel(plan_ref, table_ref, out_ref):
    zh = lax.axis_index("zh")
    here = lax.axis_index("core") * Y + lax.axis_index("y")
    bulk = EIGHTHS * 2 * CB
    row = lax.broadcasted_iota(jnp.int32, (EXTRA, LANES), 0)

    def fetch(block):
        block = jnp.clip(block, 0, 2 * PAIRS - 1)
        place = (((block >> 1) & 1) << 2) | (block >> 4)
        column = (block >> 2) & (ZH - 1)
        start = pl.multiple_of(((place << 1) | (block & 1)) * CB, CB)
        data = table_ref[column, pl.ds(start, CB)]
        lines = table_ref[column, bulk:]
        lines = jnp.where(place == here, lines, jnp.zeros_like(lines))
        return data, lines

    for index in range(CHUNKS):
        place = index % EIGHTHS
        pair = ((place % Y * ZH + zh) * CORE) + place // Y
        tile = pair * X + index // EIGHTHS
        first = plan_ref[0, 0, tile]
        data, lines = fetch(first)
        data_second, lines_second = fetch(first + plan_ref[1, 0, tile])
        out_ref[index, :CB] = data
        out_ref[index, CB : 2 * CB] = data_second
        out_ref[index, 2 * CB :] = jnp.where(row < EXTRA // 2, lines, lines_second)


def chunk_place(chunk):
    return chunk


def scales(edge_ref, first_half, second_half, zl, length):
    row = lax.broadcasted_iota(jnp.int32, (EXTRA, LANES), 0)
    other = jnp.where(row < EXTRA // 2, first_half, second_half) > 0
    blocks = []
    for part in range(TMS):
        start = 2 * CB + part % X * EXTRA
        parts = edge_ref[part // X, start : start + EXTRA].astype(jnp.float32)
        whole = parts + (pltpu.roll(parts, EXTRA - 1, axis=0) + pltpu.roll(parts, EXTRA - 2, axis=0))
        blocks.append(jnp.where(other, pltpu.roll(whole, LANES - CB, axis=1), whole))
    average = sum(blocks[1:], blocks[0]) / TMS
    squares = pltpu.roll(average, LANES // 2, axis=1)
    apart = [block - average for block in blocks]
    spread = [piece * piece for piece in apart]
    power = squares / length + sum(spread[1:], spread[0]) / TMS
    scaling = lax.rsqrt(power + 1e-05)

    def wanted(places):
        piece = apart[places[0]]
        for zone in range(1, ZL):
            piece = jnp.where(zl == zone, apart[places[zone]], piece)
        return piece

    columns = [scaling, wanted([max(zone * X - 1, 0) for zone in range(ZL)])]
    columns += [wanted([zone * X + x for zone in range(ZL)]) for x in range(X)]
    columns.append(wanted([min(zone * X + X, TMS - 1) for zone in range(ZL)]))
    lane = lax.broadcasted_iota(jnp.int32, (EXTRA, LANES), 1)
    turned = []
    for base in (0, EXTRA // 2):
        packed = jnp.zeros((EXTRA, LANES), jnp.float32)
        for place, column in enumerate(columns):
            packed = jnp.where(row == place, column[base : base + 1], packed)
        turned.append(jnp.where(lane < CB, packed, 0.0))
    filler = jnp.zeros((LANES - 2 * EXTRA, LANES), jnp.float32)
    turned = jnp.transpose(jnp.concatenate(turned + [filler], axis=0))
    return turned[:CB, :EXTRA], turned[:CB, EXTRA : 2 * EXTRA]


def lag_kernel(length, plan_ref, data_ref, edge_ref, out_ref, wide_a, wide_b):
    zl = lax.axis_index("zl")
    pair = (lax.axis_index("y") * ZH + lax.axis_index("zh")) * CORE + lax.axis_index("core")
    tile = pair * X + lax.axis_index("x")
    alive = plan_ref[2, 0, tile]
    first_half = plan_ref[0, 0, tile] & 1
    second_half = (plan_ref[0, 0, tile] + plan_ref[1, 0, tile]) & 1
    width = (CHUNKS + 1) * LANES
    factor = 1.0 / math.sqrt(length * TMS)

    @pl.when(alive <= 0)
    def _():
        out_ref[...] = jnp.zeros_like(out_ref)

    @pl.when(alive > 0)
    def _():
        lane = lax.broadcasted_iota(jnp.int32, (CB, LANES), 1)
        zero = jnp.zeros((CB, LANES), jnp.bfloat16)
        first_scale, second_scale = scales(edge_ref, first_half, second_half, zl, length)

        first_by = first_scale[:, 0:1] * factor
        second_by = second_scale[:, 0:1]

        def white(piece, scale, column, by):
            shifted = piece.astype(jnp.float32) + scale[:, column + 2 : column + 3]
            return (shifted * by).astype(jnp.bfloat16)

        def first_chunk(chunk):
            return white(data_ref[chunk_place(chunk), :CB], first_scale, chunk // EIGHTHS, first_by)

        def second_chunk(chunk):
            if chunk < 0:
                piece = white(edge_ref[jnp.maximum(zl - 1, 0), CB : 2 * CB], second_scale, -1, second_by)
                return jnp.where(zl > 0, piece, zero)
            if chunk >= CHUNKS:
                piece = white(edge_ref[jnp.minimum(zl + 1, ZL - 1), :CB], second_scale, X, second_by)
                return jnp.where(zl < ZL - 1, piece, zero)
            return white(data_ref[chunk_place(chunk), CB : 2 * CB], second_scale, chunk // EIGHTHS, second_by)

        here = zero
        for chunk in range(CHUNKS + 1):
            past = here
            here = first_chunk(chunk) if chunk < CHUNKS else zero
            for step in range(MEDIUM):
                shift = step * FINE
                mixed = jnp.where(lane < LANES - shift, here, past)
                turned = pltpu.roll(mixed, shift, axis=1) if shift else here
                wide_a[step * CB : (step + 1) * CB, chunk * LANES : (chunk + 1) * LANES] = turned
        later = second_chunk(-1)
        for chunk in range(-1, CHUNKS + 1):
            here = later
            later = second_chunk(chunk + 1) if chunk < CHUNKS else zero
            for step in range(FINE):
                mixed = jnp.where(lane >= step, here, later)
                turned = pltpu.roll(mixed, LANES - step, axis=1) if step else here
                wide_b[
                    step * CB : (step + 1) * CB, (chunk + 1) * LANES : (chunk + 2) * LANES
                ] = turned
        for half in range(2):
            result = lax.dot_general(
                wide_a[...],
                wide_b[:, half * LANES : half * LANES + width],
                (((1,), (1,)), ((), ())),
                preferred_element_type=jnp.float32,
            )
            rounded = result.astype(jnp.bfloat16)
            for part in range(TMS // 2):
                out_ref[half * (TMS // 2) + part] = rounded[part * 2 * CB : (part + 1) * 2 * CB]


def finish_kernel(got_ref, out_hbm, out_ref, grid_ref, turn_ref, sems):
    lane = lax.broadcasted_iota(jnp.int32, (8, LANES), 1)
    copies = []
    for slot in range(X):
        total = got_ref[slot].astype(jnp.float32)
        for zl in range(1, ZL):
            total = total + got_ref[zl * X + slot].astype(jnp.float32)
        for g in range(2):
            grid_ref[g * 2 * CB : (g + 1) * 2 * CB] = total[:, g * LANES : (g + 1) * LANES]
        for half in range(2):
            parts = [
                [
                    grid_ref[pl.ds((2 * g + half) * CB + r, 8, stride=4), :]
                    for g in range(2)
                ]
                for r in range(4)
            ]
            for q in range(FINE):
                line = None
                for r in range(4):
                    piece = parts[r][q // 4]
                    shift = (CB * (r - q % 4)) % LANES
                    piece = pltpu.roll(piece, shift, axis=1) if shift else piece
                    line = piece if line is None else jnp.where(lane >= r * CB, piece, line)
                turn_ref[q * 8 : (q + 1) * 8, :] = line
            for k in range(8):
                out_ref[slot, half * 8 : half * 8 + 8, k * LANES : (k + 1) * LANES] = turn_ref[
                    pl.ds(k, 8, stride=8), :
                ]
        copies.append(pltpu.make_async_copy(out_ref.at[slot], out_hbm.at[slot], sems.at[slot]))
        copies[-1].start()
    for copy in copies:
        copy.wait()


def body(samples, tile_rows, tile_offsets, tile_live):
    length = samples.shape[1]
    bf16 = jnp.bfloat16
    parts, lines, plan = pl.pallas_call(
        split_kernel,
        out_shape=(
            jax.ShapeDtypeStruct((EIGHTHS, 2 * CB, LANES), bf16),
            jax.ShapeDtypeStruct((EXTRA, LANES), bf16),
            pltpu.SMEM((3, 1, LANES), jnp.int32),
        ),
        in_specs=[HBM] * 4,
        out_specs=(VMEM, VMEM, SMEM),
        scratch_shapes=[
            pltpu.VMEM(samples.shape, jnp.float32),
            pltpu.SemaphoreType.DMA((STRIPS + 3,)),
        ],
        compiler_params=pltpu.CompilerParams(vmem_limit_bytes=3 * MIB),
        name="split",
    )(
        *(
            pltpu.with_memory_space_constraint(array, pltpu.HBM)
            for array in (samples, tile_rows[None], tile_offsets[None], tile_live[None])
        )
    )
    with jax.named_scope("spread_y"):
        table = lax.all_to_all(parts, ("core", "y"), 0, 0, tiled=True)
    with jax.named_scope("spread_z"):
        table = jnp.concatenate([table.reshape(EIGHTHS * 2 * CB, LANES), lines])
        table = lax.all_gather(table, "zh")
    chosen = pl.pallas_call(
        select_kernel,
        out_shape=jax.ShapeDtypeStruct((CHUNKS, ROWS, LANES), bf16),
        in_specs=[SMEM, VMEM],
        out_specs=VMEM,
        compiler_params=pltpu.CompilerParams(vmem_limit_bytes=6 * MIB),
        name="select",
    )(pltpu.with_memory_space_constraint(plan, pltpu.SMEM), table)
    with jax.named_scope("collect"):
        data = lax.all_to_all(chosen, ("x", "core", "y"), 0, 0, tiled=True)
    with jax.named_scope("edges"):
        sums = jnp.sum(data[:, 2 * CB :].reshape(X, EIGHTHS, EXTRA, LANES), axis=1)
        sums = sums.reshape(X * EXTRA, LANES)
        edges = jnp.concatenate(
            [data[chunk_place(0), CB : 2 * CB], data[chunk_place(CHUNKS - 1), CB : 2 * CB], sums]
        )
        edges = lax.all_to_all(
            jnp.broadcast_to(edges[None], (ZL,) + edges.shape), "zl", 0, 0, tiled=True
        )
    partial = pl.pallas_call(
        lambda *refs: lag_kernel(length, *refs),
        out_shape=jax.ShapeDtypeStruct((TMS, 2 * CB, FINE * CB), bf16),
        in_specs=[SMEM, VMEM, VMEM],
        out_specs=VMEM,
        scratch_shapes=[
            pltpu.VMEM((MEDIUM * CB, (CHUNKS + 1) * LANES), bf16),
            pltpu.VMEM((FINE * CB, (CHUNKS + 2) * LANES), bf16),
        ],
        compiler_params=pltpu.CompilerParams(vmem_limit_bytes=16 * MIB),
        name="lags",
    )(pltpu.with_memory_space_constraint(plan, pltpu.SMEM), data, edges)
    with jax.named_scope("reduce"):
        got = lax.all_to_all(partial, ("zl", "x"), 0, 0, tiled=True)
    return pl.pallas_call(
        finish_kernel,
        out_shape=jax.ShapeDtypeStruct((X, 2 * FINE, CB * CB), jnp.float32),
        in_specs=[VMEM],
        out_specs=HBM,
        scratch_shapes=[
            pltpu.VMEM((X, 2 * FINE, CB * CB), jnp.float32),
            pltpu.VMEM((4 * CB, LANES), jnp.float32),
            pltpu.VMEM((FINE * 8, LANES), jnp.float32),
            pltpu.SemaphoreType.DMA((X,)),
        ],
        compiler_params=pltpu.CompilerParams(vmem_limit_bytes=4 * MIB),
        name="finish",
    )(got)


def solution(mesh):
    devices = mesh.devices.reshape(Y, ZH, CORE, ZL, X)
    spread = Mesh(devices, AXES)
    pair, tm = ("y", "zh", "core"), ("zl", "x")
    return jax.shard_map(
        body,
        mesh=spread,
        in_specs=(P(pair, tm), P(), P(), P()),
        out_specs=P(pair, tm, None),
        check_vma=False,
    )
```
